256 devices in a mesh: lat: 16 (over x, y), lon: 16 (over z, core).
Axes of the slice: x: 4, y: 4, z: 8, core: 2. Of those that a mesh axis runs over, the one named last changes fastest.
Arguments:
- start_block: float32 [512, 8, 2, 1025], P(('lat', 'lon')), may hold values from -6 to 6
- legendre: bfloat16 [512, 1024, 1025], P('lat', 'lon'), may hold values from -0.1875 to 0.1875
- variance: float32 [1024, 2048], P('lon', 'lat'), may hold values from 0.25 to 4
- gauss_weight: float32 [1024], P('lon'), may hold values from 0.1 to 1.9
- pair_of_slot: int32 [512], replicated, may hold values from 0 to 511, each once
Outputs:
- modes: float32 [512, 8, 2, 1025], P(('lat', 'lon'))
- factor: float32 [8, 8], replicated
The draws below stay inside these ranges and needn't reach their ends.
Inputs may be any that keep to these rules, and one draw needn't show every extreme that they name: `pair_of_slot`: each pair number appears in exactly one slot.
All inputs are finite; a program needn't handle non-finite values.
Results may differ from the reference program's by a relative error of at most 0.025.
Values may be sent and summed in bfloat16 or wider, within the bound.
No kernel may reach another device: no remote copies, remote signals or barrier semaphores. Data moves between devices by JAX's collectives and lax.ppermute only.
A program may use at most 64 MiB of HBM per device.

```python
import math
import jax
import jax.numpy as jnp
from jax import lax

T_SIZE = 1023
NLAT = 1024
NLON = 2048
K = 8
STEPS = 3
NPAIR = 512
R = 1025


def levels(key, dims, split, low, high):
    gain, own = 1.0, jax.random.fold_in(key, 6)
    for position, shards_of in split:
        heights = jnp.exp(jax.random.uniform(jax.random.fold_in(own, position), (shards_of,), jnp.float32, low / len(split), high / len(split)))
        gain = gain * jnp.repeat(heights, dims[position] // shards_of).reshape([-1 if axis == position else 1 for axis in range(len(dims))])
    return gain


def bell_draw(stream_key, extent, deviation, limit, pieces=(), kind=jnp.bfloat16):
    gain = levels(stream_key, extent, pieces, -0.22, 0.18) if pieces else 1.0
    array = jax.random.normal(stream_key, extent, jnp.float32) * deviation * gain
    return jnp.minimum(jnp.maximum(array, -limit), limit).astype(kind)


def setup_inputs(seed: int = 0) -> dict:
    keys = jax.random.split(jax.random.key(seed), 6)
    return {
        "start_block": bell_draw(keys[0], (NPAIR, K, 2, R), 1.0, 6.0, ((0, 256),), jnp.float32),
        "legendre": bell_draw(keys[1], (NPAIR, NLAT, R), R ** -0.5, 0.1875, ((0, 16), (1, 16))),
        "variance": jnp.clip(jnp.exp(math.log(4.0) - 2.7725887 * jax.random.uniform(keys[2], (NLAT, NLON), jnp.float32) ** levels(keys[2], (NLAT, NLON), ((0, 16), (1, 16)), -0.2, 0.2)), 0.25, 4.0),
        "gauss_weight": jnp.clip(1.0 + 0.18 * jax.random.normal(keys[3], (NLAT,), jnp.float32), 0.1, 1.9),
        "pair_of_slot": jax.random.permutation(keys[4], NPAIR).astype(jnp.int32),
    }


def pair_layout(pair_ids, width):
    places = jnp.arange(width, dtype=jnp.int32)
    cut = T_SIZE + 1 - pair_ids
    first = places[None, :] < cut[:, None]
    degree = jnp.where(first, pair_ids[:, None] + places[None, :], places[None, :] - 1)
    return (first, degree)

def spectral_factor(degree):
    level = degree.astype(jnp.float32)
    return lax.rsqrt(1.0 + level * (level + 1.0) * (4.0 / (T_SIZE * T_SIZE)))

def wave_angles(pair_ids, lon_ids):
    waves = jnp.stack([pair_ids, T_SIZE - pair_ids], axis=1)
    phase = waves[:, :, None] * lon_ids[None, None, :] % NLON
    return (waves, phase.astype(jnp.float32) * (2.0 * math.pi / NLON))

def inverse_table(pair_ids, lon_ids):
    waves, angle = wave_angles(pair_ids, lon_ids)
    weight = jnp.where(waves == 0, 1.0, 2.0).astype(jnp.float32)[:, :, None, None]
    return (weight * jnp.stack([jnp.cos(angle), -jnp.sin(angle)], axis=2)).astype(jnp.bfloat16)

def forward_table(pair_ids, lon_ids):
    waves, angle = wave_angles(pair_ids, lon_ids)
    return (jnp.stack([jnp.cos(angle), -jnp.sin(angle)], axis=2) * (1.0 / NLON)).astype(jnp.bfloat16)

def orthonormal(shaped):
    gram = jnp.einsum('skcr,sqcr->kq', shaped, shaped, precision=lax.Precision.HIGHEST) / (2.0 * NPAIR * R)
    lower = jnp.linalg.cholesky(gram)
    inverse = jax.scipy.linalg.solve_triangular(lower, jnp.eye(K, dtype=jnp.float32), lower=True)
    current = jnp.einsum('kq,sqcr->skcr', inverse, shaped, precision=lax.Precision.HIGHEST)
    return (lower, current)

def reference(start_block, legendre, variance, gauss_weight, pair_of_slot):
    first, degree = pair_layout(pair_of_slot, R)
    factor_rows = spectral_factor(degree)
    lon_ids = jnp.arange(NLON, dtype=jnp.int32)
    inv_tab = inverse_table(pair_of_slot, lon_ids).astype(jnp.float32)
    fwd_tab = forward_table(pair_of_slot, lon_ids).astype(jnp.float32)
    current = start_block
    lower = jnp.zeros((K, K), jnp.float32)
    for step in range(STEPS):
        spec = current.astype(jnp.bfloat16)
        mask = first[:, None, None, :]
        masked = jnp.stack([jnp.where(mask, spec, 0), jnp.where(mask, 0, spec)], axis=1)
        masked = masked.reshape(NPAIR, 4 * K, R)

        def inverse_one(pair):
            return jnp.dot(pair[0].astype(jnp.float32), pair[1].astype(jnp.float32).T, precision=lax.Precision.HIGHEST)
        waves = lax.map(inverse_one, (masked, legendre)).astype(jnp.bfloat16)
        waves = waves.reshape(NPAIR, 2, K, 2, NLAT).astype(jnp.float32)
        grid = jnp.einsum('shkcj,shcl->kjl', waves, inv_tab, precision=lax.Precision.HIGHEST)
        scaled_grid = (grid * variance[None]).astype(jnp.bfloat16).astype(jnp.float32)
        summed = jnp.einsum('kjl,shcl->shkcj', scaled_grid, fwd_tab, precision=lax.Precision.HIGHEST)
        spectral_grid = (summed * gauss_weight[None, None, None, None, :]).astype(jnp.bfloat16)
        flat = spectral_grid.reshape(NPAIR, 4 * K, NLAT)

        def forward_one(pair):
            return jnp.dot(pair[0].astype(jnp.float32), pair[1].astype(jnp.float32), precision=lax.Precision.HIGHEST)
        projected = lax.map(forward_one, (flat, legendre)).reshape(NPAIR, 2, K, 2, R)
        projected = jnp.where(mask, projected[:, 0], projected[:, 1])
        shaped = projected * factor_rows[:, None, None, :]
        lower, current = orthonormal(shaped)
    return (current, lower)
```

```python
import functools
import math

import jax
import jax.numpy as jnp
import numpy as np
from jax import lax
from jax.experimental import pallas as pl
from jax.experimental.pallas import tpu as pltpu
from jax.sharding import Mesh
from jax.sharding import PartitionSpec as P

T_SIZE = 1023
NLON = 2048
K = 8
STEPS = 3
NPAIR = 512
R = 1025
RP = 1152
BF = jnp.bfloat16
F32 = jnp.float32
GSCALE = 1.0 / (2.0 * NPAIR * R)
SIGNS = np.array([[1, 1, 1, 1], [1, -1, 1, -1], [1, -1, -1, 1], [1, 1, -1, -1]], np.float32)


def natural_tables():
    q = np.arange(512)[:, None]
    i2 = 2 * np.arange(512)[None, :] + 1
    out = []
    for m in (2 * q, 1023 - 2 * q):
        angle = (m * i2 % 4096) * (2.0 * math.pi / 4096)
        out += [np.cos(angle), np.sin(angle)]
    return np.stack(out).astype(jnp.bfloat16)


def fold_matrix():
    f = np.zeros((4, 4, K, 4, 4, 4, K), np.float32)
    for jj in range(4):
        for g in range(4):
            for q in range(4):
                f[jj, g, :, g, q, jj, :] = SIGNS[g, q]
    return f.reshape(128, 512)


def lanes(shape):
    return lax.broadcasted_iota(jnp.int32, shape, len(shape) - 1)


def rows(shape):
    return lax.broadcasted_iota(jnp.int32, shape, len(shape) - 2)


def split_tile(g):
    hi = g.astype(BF).astype(F32)
    rest = g - hi
    mid = rest.astype(BF).astype(F32)
    low = (rest - mid).astype(BF).astype(F32)
    return hi + pltpu.roll(mid, 8, 1) + pltpu.roll(low, 16, 1)


def join_tile(t):
    g = t + pltpu.roll(t, 120, 1) + pltpu.roll(t, 112, 1)
    lane = lanes(t.shape)
    return jnp.where((lane >= 8) & (lane < 16) & (rows(t.shape) < 8), g, 0.0)


def eliminate(gram):
    lane, row = lanes((16, 128)), rows((16, 128))
    a = jnp.where(row < 8, gram * GSCALE, jnp.where(row - 8 == lane, 1.0, 0.0))
    scale = jnp.zeros((1, 128), F32)
    lane1 = lanes((1, 128))
    for p in range(K):
        prow = a[p : p + 1, :]
        piv = jnp.sum(jnp.where(lane1 == p, prow, 0.0), axis=1, keepdims=True)
        scale = jnp.where(lane1 == p, lax.rsqrt(piv), scale)
        if p < K - 1:
            col = jnp.sum(jnp.where(lane == p, a, 0.0), axis=1, keepdims=True)
            a = a - jnp.where(lane > p, col * (prow / piv), 0.0)
    return a * scale


def even_mask(shape, pid):
    first = (lanes(shape) < T_SIZE + 1 - pid).astype(jnp.int32)
    return first != lax.rem(pid, 2)


def inverse_kernel(with_gram, pid_ref, spec_ref, leg_ref, out_ref, acc_ref):
    step = pl.program_id(0)
    per = leg_ref.shape[0]
    lane = lanes((32, 128))
    for t in range(per):
        sp = spec_ref[t // 2, 16 * (t % 2) : 16 * (t % 2) + 16, :].astype(F32)
        mask = even_mask((16, RP), pid_ref[step * per + t])
        even = jnp.where(mask, sp, 0.0).astype(BF)
        odd = jnp.where(mask, 0.0, sp).astype(BF)
        wide = jnp.concatenate([even, odd] * 4, axis=0)
        p = lax.dot_general(leg_ref[t], wide, (((1,), (1,)), ((), ())), preferred_element_type=F32)
        o = jnp.where(lane < 32, p[0:32], jnp.where(lane < 64, p[32:64], jnp.where(lane < 96, p[64:96], p[96:128])))
        acc_ref[:, step * per + t, :] = o
    if with_gram:

        @pl.when(step == 0)
        def _():
            acc_ref[:, 16:32, :] = jnp.zeros((32, 16, 128), F32)

        tile = spec_ref[0, 0:16, 1024:RP].astype(F32)
        for z in range(1, spec_ref.shape[0]):
            tile = tile + spec_ref[z, 0:16, 1024:RP].astype(F32)
        g = join_tile(tile)
        acc_ref[0, 16:32, :] += g

    @pl.when(step == pl.num_programs(0) - 1)
    def _():
        out_ref[:, 0:16, :] = acc_ref[:, 0:16, :].astype(BF)
        if with_gram:
            t = split_tile(acc_ref[0, 16:32, :]).astype(BF)
            out_ref[:, 16:32, :] = jnp.broadcast_to(t[None], (32, 16, 128))


def legendre_inverse(spec, leg, pid16, with_gram):
    height = 32 if with_gram else 16
    return pl.pallas_call(
        functools.partial(inverse_kernel, with_gram),
        grid=(4,),
        in_specs=[
            pl.BlockSpec(memory_space=pltpu.SMEM),
            pl.BlockSpec((2, 32, RP), lambda i: (i, 0, 0)),
            pl.BlockSpec((4, 128, RP), lambda i: (i, 0, 0)),
        ],
        out_specs=pl.BlockSpec((32, height, 128), lambda i: (0, 0, 0)),
        out_shape=jax.ShapeDtypeStruct((32, height, 128), BF),
        scratch_shapes=[pltpu.VMEM((32, height, 128), F32)],
        compiler_params=pltpu.CompilerParams(vmem_limit_bytes=24 << 20),
    )(pid16, spec, leg)


def grid_kernel(with_gram, x_ref, fold_ref, tt_ref, t_ref, var_ref, y_ref, hat_ref):
    x = x_ref[:, 0:16, :].reshape(512, 128)
    if with_gram:
        tile = jnp.sum(x_ref[:, 16:32, :].astype(F32), axis=0)
        gram = pltpu.roll(join_tile(tile), 120, 1)
        mix = jnp.where(lanes((8, 128)) < 8, eliminate(gram)[8:16, :], 0.0)
        for shift in (8, 16, 32, 64):
            mix = mix + pltpu.roll(mix, shift, 1)
        mix = jnp.concatenate([mix] * 16, axis=0)
    for g in range(4):
        f = fold_ref[:, 128 * g : 128 * g + 128].astype(F32)
        if with_gram:
            f = f * mix
            hi = f.astype(BF)
            low = (f - hi.astype(F32)).astype(BF)
            hat = jnp.dot(x, hi, preferred_element_type=F32) + jnp.dot(x, low, preferred_element_type=F32)
        else:
            f = jnp.where(lax.rem(rows((128, 128)), 8) == lax.rem(lanes((128, 128)), 8), f, 0.0)
            hat = jnp.dot(x, f.astype(BF), preferred_element_type=F32)
        hat_ref[512 * g : 512 * g + 512, :] = hat.astype(BF)
    grid = jnp.dot(tt_ref[...], hat_ref[...], preferred_element_type=F32)
    scaled = (grid * var_ref[...]).astype(BF)
    lane = lanes((1, 128))
    out = None
    for g in range(4):
        part = jnp.dot(t_ref[512 * g : 512 * g + 512, :], scaled, preferred_element_type=F32)
        sign = jnp.ones((1, 128), F32)
        for q in range(4):
            if SIGNS[g, q] < 0:
                sign = jnp.where((lane >= 32 * q) & (lane < 32 * q + 32), -1.0, sign)
        part = part * sign
        part = part + pltpu.roll(part, 64, 1)
        part = part + pltpu.roll(part, 32, 1)
        out = part if out is None else jnp.where(lane >= 32 * g, part, out)
    y_ref[...] = out.astype(BF).reshape(32, 16, 128)


def grid_stage(x, fold, tt, t, var, with_gram):
    return pl.pallas_call(
        functools.partial(grid_kernel, with_gram),
        out_shape=jax.ShapeDtypeStruct((32, 16, 128), BF),
        scratch_shapes=[pltpu.VMEM((2048, 128), BF)],
        compiler_params=pltpu.CompilerParams(vmem_limit_bytes=32 << 20),
    )(x, fold, tt, t, var)


def forward_kernel(pid_ref, y_ref, leg_ref, out_ref, wide_ref, lhs_ref):
    step = pl.program_id(0)
    per = leg_ref.shape[0]

    @pl.when(step == 0)
    def _():
        wide_ref[...] = y_ref[...].astype(F32)
        lane = lanes((32, 128))
        for b in range(4):
            z = jnp.concatenate([wide_ref[:, 4 * b + s, :] for s in range(4)], axis=0)
            zt = z.T
            blocks = [
                jnp.concatenate([zt[32 * g + 8 * jj : 32 * g + 8 * jj + 8, :] for g in range(4)], axis=0)
                for jj in range(4)
            ]
            for s in range(4):
                o = None
                for jj in range(4):
                    shift = (32 * (jj - s)) % 128
                    v = pltpu.roll(blocks[jj], shift, 1) if shift else blocks[jj]
                    o = v if o is None else jnp.where(lane >= 32 * jj, v, o)
                lhs_ref[4 * b + s] = o.astype(BF)

    for t in range(per):
        p = jnp.dot(lhs_ref[step * per + t], leg_ref[t], preferred_element_type=F32)
        mask = even_mask((16, RP), pid_ref[step * per + t])
        out_ref[t // 2, 16 * (t % 2) : 16 * (t % 2) + 16, :] = jnp.where(mask, p[0:16], p[16:32]).astype(BF)


def legendre_forward(y, leg, pid16):
    return pl.pallas_call(
        forward_kernel,
        grid=(4,),
        in_specs=[
            pl.BlockSpec(memory_space=pltpu.SMEM),
            pl.BlockSpec((32, 16, 128), lambda i: (0, 0, 0)),
            pl.BlockSpec((4, 128, RP), lambda i: (i, 0, 0)),
        ],
        out_specs=pl.BlockSpec((2, 32, RP), lambda i: (i, 0, 0)),
        out_shape=jax.ShapeDtypeStruct((8, 32, RP), BF),
        scratch_shapes=[pltpu.VMEM((32, 16, 128), F32), pltpu.VMEM((16, 32, 128), BF)],
        compiler_params=pltpu.CompilerParams(vmem_limit_bytes=24 << 20),
    )(pid16, y, leg)


def gram_tile(sh):
    hi = sh.astype(BF)
    low = (sh - hi.astype(F32)).astype(BF)
    both = jnp.concatenate([hi, low], axis=0)
    pad = jnp.concatenate([both, jnp.zeros((64, RP), BF)], axis=0)
    full = lax.dot_general(both, pad, (((1,), (1,)), ((), ())), preferred_element_type=F32)
    total = None
    for a in range(2):
        for b in range(2):
            for i in range(4):
                v = full[32 * a + 8 * i : 32 * a + 8 * i + 8, :]
                shift = (128 - (32 * b + 8 * i)) % 128
                v = pltpu.roll(v, shift, 1) if shift else v
                total = v if total is None else total + v
    return jnp.where(lanes((8, 128)) < 8, total, 0.0)


def summed_block(parts_ref, scale_ref):
    total = parts_ref[0].astype(F32)
    for z in range(1, parts_ref.shape[0]):
        total = total + parts_ref[z].astype(F32)
    scale = jnp.concatenate([jnp.broadcast_to(scale_ref[b : b + 1, :], (16, RP)) for b in range(2)], axis=0)
    return total * scale


def owner_kernel(parts_ref, scale_ref, weight_ref, out_ref):
    sh = summed_block(parts_ref, scale_ref)
    gram = gram_tile(sh)
    weight = jnp.concatenate([jnp.broadcast_to(weight_ref[b : b + 1, :], (16, RP)) for b in range(2)], axis=0)
    spec = (sh * weight).astype(BF)
    tile = split_tile(pltpu.roll(gram, 8, 1))
    tile = jnp.concatenate([tile, jnp.zeros((24, 128), F32)], axis=0)
    last = jnp.where(lanes((32, 128)) == 0, spec[:, 1024:RP].astype(F32), tile).astype(BF)
    for z in range(out_ref.shape[0]):
        out_ref[z, :, 0:1024] = spec[:, 0:1024]
        out_ref[z, :, 1024:RP] = last


def owner_step(parts, scale, weight):
    return pl.pallas_call(
        owner_kernel,
        out_shape=jax.ShapeDtypeStruct((8, 32, RP), BF),
        compiler_params=pltpu.CompilerParams(vmem_limit_bytes=24 << 20),
    )(parts, scale, weight)


def last_kernel(parts_ref, scale_ref, sh_ref, gram_ref):
    sh = summed_block(parts_ref, scale_ref)
    sh_ref[...] = sh
    gram_ref[...] = gram_tile(sh)


def last_step(parts, scale):
    return pl.pallas_call(
        last_kernel,
        out_shape=(jax.ShapeDtypeStruct((32, RP), F32), jax.ShapeDtypeStruct((8, 128), F32)),
        compiler_params=pltpu.CompilerParams(vmem_limit_bytes=24 << 20),
    )(parts, scale)


def finish_kernel(sh_ref, gram_ref, cos_ref, sin_ref, modes_ref, lower_ref):
    rowsum = gram_ref[0:8, :]
    for i in range(1, gram_ref.shape[0] // 8):
        rowsum = rowsum + gram_ref[8 * i : 8 * i + 8, :]
    both = eliminate(jnp.concatenate([rowsum, jnp.zeros((8, 128), F32)], axis=0))
    lower_ref[...] = jnp.where(lanes((8, 128)) <= rows((8, 128)), both[0:8, :], 0.0)
    mix = both[8:16, :]
    for b in range(2):
        cos, sin = cos_ref[b : b + 1, :], sin_ref[b : b + 1, :]
        parts = []
        for c in range(2):
            block = sh_ref[16 * b + 8 * c : 16 * b + 8 * c + 8, :]
            out = jnp.zeros((8, RP), F32)
            for q in range(K):
                coef = jnp.sum(jnp.where(rows((8, 8)) == lanes((8, 8)), jnp.broadcast_to(mix[q : q + 1, 0:8], (8, 8)), 0.0), axis=1, keepdims=True)
                out = out + coef * block[q : q + 1, :]
            parts.append(out)
        modes_ref[b, 0] = cos * parts[0] + sin * parts[1]
        modes_ref[b, 1] = sin * parts[0] - cos * parts[1]


def finish(sh, grams, cos, sin):
    return pl.pallas_call(
        finish_kernel,
        out_shape=(jax.ShapeDtypeStruct((2, 2, K, RP), F32), jax.ShapeDtypeStruct((8, 128), F32)),
        compiler_params=pltpu.CompilerParams(vmem_limit_bytes=24 << 20),
    )(sh, grams, cos, sin)


def owner_tables(pid2):
    places = jnp.arange(RP, dtype=jnp.int32)[None, :]
    pid = pid2[:, None]
    first = places < T_SIZE + 1 - pid
    degree = jnp.where(first, pid + places, places - 1)
    wave = jnp.where(first, pid, T_SIZE - pid)
    level = degree.astype(F32)
    scale = lax.rsqrt(1.0 + level * (level + 1.0) * (4.0 / (T_SIZE * T_SIZE)))
    scale = jnp.where(places < R, scale * (1.0 / NLON), 0.0)
    weight = jnp.where(wave == 0, 1.0, 2.0).astype(F32)
    phase = wave.astype(F32) * (2.0 * math.pi / (2 * NLON))
    return scale, weight, jnp.cos(phase), jnp.sin(phase)


def body(start_block, legendre, variance, gauss_weight, pair_of_slot):
    lat, zpos, core = lax.axis_index("lat"), lax.axis_index("z"), lax.axis_index("c")
    pids = pair_of_slot.reshape(16, 8, 2, 2)
    pid2 = lax.dynamic_slice(pids, (lat, zpos, core, 0), (1, 1, 1, 2)).reshape(2)
    pid16 = lax.dynamic_slice(pids, (lat, 0, core, 0), (1, 8, 1, 2)).reshape(16)
    pid_recv = pids.transpose(0, 2, 1, 3).reshape(512)

    leg = legendre.reshape(8, 2, 2, 64, R)
    other = lax.dynamic_slice_in_dim(leg, 1 - core, 1, 1)
    mine = lax.dynamic_slice_in_dim(leg, core, 1, 1)
    got = lax.ppermute(other, "c", [(0, 1), (1, 0)])
    both = jnp.where(core == 0, jnp.stack([mine, got], axis=3), jnp.stack([got, mine], axis=3))
    both = jnp.pad(both.reshape(16, 128, R), ((0, 0), (0, 0), (0, RP - R)))

    var = variance * gauss_weight[:, None]
    var = var.reshape(2, 32, 128).transpose(1, 0, 2)
    var = lax.all_to_all(var, ("lat", "c"), 0, 0, tiled=True)
    var = var.reshape(16, 4, 128).transpose(1, 0, 2).reshape(4, 4, 512)
    var = jnp.stack([var[:, 0], var[:, 1, ::-1], var[:, 2], var[:, 3, ::-1]], axis=0)
    var = jnp.repeat(var.reshape(16, 512).T, K, axis=1)

    place = jnp.where(pid_recv % 2 == 0, pid_recv, T_SIZE - pid_recv) // 2
    nat = natural_tables()
    hot = (place[:, None] == jnp.arange(512, dtype=jnp.int32)[None, :]).astype(BF)
    t = jnp.einsum("sq,gqi->gsi", hot, jnp.asarray(nat), preferred_element_type=F32).astype(BF).reshape(2048, 512)
    nat_t = np.ascontiguousarray(nat.transpose(2, 0, 1))
    tt = jnp.einsum("igq,sq->igs", jnp.asarray(nat_t), hot, preferred_element_type=F32).astype(BF).reshape(512, 2048)
    fold = jnp.asarray(fold_matrix(), BF)

    scale, weight, cos, sin = owner_tables(pid2)
    start = jnp.pad(start_block, ((0, 0), (0, 0), (0, 0), (0, RP - R)))
    re, im = start[:, :, 0, :], start[:, :, 1, :]
    cb, sb, wb = cos[:, None, :], sin[:, None, :], weight[:, None, :]
    spec = jnp.stack([wb * (re * cb + im * sb), wb * (re * sb - im * cb)], axis=1).astype(BF)
    spec = jnp.broadcast_to(spec.reshape(1, 32, RP), (8, 32, RP))

    for step in range(STEPS):
        spec = lax.all_to_all(spec, "z", 0, 0, tiled=True)
        x = legendre_inverse(spec, both, pid16, step > 0)
        x = lax.all_to_all(x, ("lat", "c"), 0, 0, tiled=True)
        y = grid_stage(x, fold, tt, t, var, step > 0)
        y = lax.all_to_all(y, ("lat", "c"), 0, 0, tiled=True)
        parts = legendre_forward(y, both, pid16)
        parts = lax.all_to_all(parts, "z", 0, 0, tiled=True)
        if step + 1 < STEPS:
            spec = owner_step(parts, scale, weight)
    sh, gram = last_step(parts, scale)
    grams = lax.all_to_all(jnp.broadcast_to(gram[None, :, 0:8].reshape(1, 64), (256, 64)), ("lat", "z", "c"), 0, 0, tiled=True)
    total = jnp.sum(grams, axis=0).reshape(8, 8)
    modes, lower = finish(sh, jnp.pad(total, ((0, 0), (0, 120))), cos, sin)
    return modes.transpose(0, 2, 1, 3)[:, :, :, :R], lower[:, :K]


def solution(mesh):
    fine = Mesh(mesh.devices.reshape(16, 8, 2), ("lat", "z", "c"))
    placed = (
        P(("lat", "z", "c"), None, None, None),
        P("lat", ("z", "c"), None),
        P(("z", "c"), "lat"),
        P(("z", "c")),
        P(),
    )
    return jax.shard_map(
        body,
        mesh=fine,
        in_specs=placed,
        out_specs=(P(("lat", "z", "c"), None, None, None), P()),
        check_vma=False,
    )
```

```python
import functools
import math

import jax
import jax.numpy as jnp
import numpy as np
from jax import lax
from jax.experimental import pallas as pl
from jax.experimental.pallas import tpu as pltpu
from jax.sharding import Mesh
from jax.sharding import PartitionSpec as P

T_SIZE = 1023
NLON = 2048
K = 8
STEPS = 3
NPAIR = 512
R = 1025
RP = 1152
BF = jnp.bfloat16
F32 = jnp.float32
GSCALE = 1.0 / (2.0 * NPAIR * R)
SIGNS = np.array([[1, 1, 1, 1], [1, -1, 1, -1], [1, -1, -1, 1], [1, 1, -1, -1]], np.float32)


def natural_tables():
    q = np.arange(512)[:, None]
    i2 = 2 * np.arange(512)[None, :] + 1
    out = []
    for m in (2 * q, 1023 - 2 * q):
        angle = (m * i2 % 4096) * (2.0 * math.pi / 4096)
        out += [np.cos(angle), np.sin(angle)]
    return np.stack(out).astype(jnp.bfloat16)


def fold_matrix():
    f = np.zeros((4, 4, K, 4, 4, 4, K), np.float32)
    for jj in range(4):
        for g in range(4):
            for q in range(4):
                f[jj, g, :, g, q, jj, :] = SIGNS[g, q]
    return f.reshape(128, 512)


def lanes(shape):
    return lax.broadcasted_iota(jnp.int32, shape, len(shape) - 1)


def rows(shape):
    return lax.broadcasted_iota(jnp.int32, shape, len(shape) - 2)


def split_tile(g):
    hi = g.astype(BF).astype(F32)
    rest = g - hi
    mid = rest.astype(BF).astype(F32)
    low = (rest - mid).astype(BF).astype(F32)
    return hi + pltpu.roll(mid, 8, 1) + pltpu.roll(low, 16, 1)


def join_tile(t):
    g = t + pltpu.roll(t, 120, 1) + pltpu.roll(t, 112, 1)
    lane = lanes(t.shape)
    return jnp.where((lane >= 8) & (lane < 16) & (rows(t.shape) < 8), g, 0.0)


def splat_factor(gram):
    g = [[jnp.broadcast_to(gram[i : i + 1, j : j + 1] * GSCALE, (8, 128)) for j in range(i + 1)] for i in range(K)]
    low = [[None] * K for _ in range(K)]
    inv = [[None] * K for _ in range(K)]
    for j in range(K):
        d = g[j][j]
        for p in range(j):
            d = d - low[j][p] * low[j][p]
        r = lax.rsqrt(d)
        r = r * (1.5 - 0.5 * d * r * r)
        low[j][j] = d * r
        inv[j][j] = r
        for i in range(j + 1, K):
            v = g[i][j]
            for p in range(j):
                v = v - low[i][p] * low[j][p]
            low[i][j] = v * r
    for j in range(K):
        for i in range(j + 1, K):
            v = low[i][j] * inv[j][j]
            for p in range(j + 1, i):
                v = v + low[i][p] * inv[p][j]
            inv[i][j] = -(v * inv[i][i])
    return low, inv


def tile_of(entries, transposed, period):
    row, lane = rows((8, 128)), lanes((8, 128))
    if period:
        lane = lax.rem(lane, period)
    out = jnp.zeros((8, 128), F32)
    for i in range(K):
        for j in range(i + 1):
            r, l = (j, i) if transposed else (i, j)
            out = jnp.where((row == r) & (lane == l), entries[i][j], out)
    return out


def even_mask(shape, pid):
    first = (lanes(shape) < T_SIZE + 1 - pid).astype(jnp.int32)
    return first != lax.rem(pid, 2)


def load_block(ref, z, b):
    main = [ref[z, (b * 8 + l) * 16 : (b * 8 + l) * 16 + 16, :].astype(F32) for l in range(8)]
    extra = ref[z, 256:272, :].astype(F32)
    if b:
        extra = pltpu.roll(extra, 128 - b, 1)
    return jnp.concatenate(main + [jnp.where(lanes((16, 128)) == 0, extra, 0.0)], axis=1)


def pack(blocks, tile):
    lane = lanes((16, 128))
    pieces = [v[:, 128 * l : 128 * l + 128].astype(BF) for v in blocks for l in range(8)]
    extra = jnp.where(lane == 0, blocks[0][:, 1024:RP], jnp.where(lane == 1, pltpu.roll(blocks[1][:, 1024:RP], 1, 1), tile))
    return pieces + [extra.astype(BF)]


def start_kernel(pid_ref, at_ref, start_ref, out_ref, table_ref):
    base = at_ref[0] + at_ref[1]
    place, row = lanes((2, RP)), rows((2, RP))
    pid = jnp.where(row == 0, pid_ref[base], pid_ref[base + 1])
    first = place < T_SIZE + 1 - pid
    degree = jnp.where(first, pid + place, place - 1)
    wave = jnp.where(first, pid, T_SIZE - pid)
    level = degree.astype(F32)
    scale = lax.rsqrt(1.0 + level * (level + 1.0) * (4.0 / (T_SIZE * T_SIZE)))
    scale = jnp.where(place < R, scale * (1.0 / NLON), 0.0)
    weight = jnp.where(wave == 0, 1.0, 2.0).astype(F32)
    phase = wave.astype(F32) * (2.0 * math.pi / (2 * NLON))
    cos, sin = jnp.cos(phase), jnp.sin(phase)
    table_ref[0:2, :] = scale
    table_ref[2:4, :] = weight
    table_ref[4:6, :] = cos
    table_ref[6:8, :] = sin
    lane = lanes((8, 128))
    blocks = []
    for b in range(2):
        half = []
        for c in range(2):
            col = jnp.broadcast_to(start_ref[b, :, c, 1024:R], (8, 128))
            half.append(jnp.concatenate([start_ref[b, :, c, 0:1024], jnp.where(lane == 0, col, 0.0)], axis=1))
        re, im = half
        cb, sb, wb = cos[b : b + 1], sin[b : b + 1], weight[b : b + 1]
        blocks.append(jnp.concatenate([wb * (re * cb + im * sb), wb * (re * sb - im * cb)], axis=0))
    pieces = pack(blocks, jnp.zeros((16, 128), F32))
    for z in range(out_ref.shape[0]):
        for n, v in enumerate(pieces):
            out_ref[z, 16 * n : 16 * n + 16, :] = v


SMEM = pl.BlockSpec(memory_space=pltpu.SMEM)
VMEM = pl.BlockSpec(memory_space=pltpu.VMEM)


def start_step(pids, at, start):
    return pl.pallas_call(
        start_kernel,
        in_specs=[SMEM, SMEM, VMEM],
        out_shape=(jax.ShapeDtypeStruct((8, 272, 128), BF), jax.ShapeDtypeStruct((8, RP), F32)),
        compiler_params=pltpu.CompilerParams(vmem_limit_bytes=12 << 20),
    )(pids, at, start)


def table_kernel(place_ref, nat_ref, natt_ref, t_ref, tt_ref):
    hot = jnp.where(rows((512, 512)) == place_ref[...], 1.0, 0.0)
    hot_s = hot.T.astype(BF)
    hot = hot.astype(BF)
    for g in range(4):
        t_ref[512 * g : 512 * g + 512, :] = jnp.dot(hot_s, nat_ref[512 * g : 512 * g + 512, :], preferred_element_type=F32).astype(BF)
        tt_ref[:, 512 * g : 512 * g + 512] = jnp.dot(natt_ref[:, 512 * g : 512 * g + 512], hot, preferred_element_type=F32).astype(BF)


def slot_tables(place):
    nat = natural_tables()
    natt = np.ascontiguousarray(nat.transpose(2, 0, 1)).reshape(512, 2048)
    return pl.pallas_call(
        table_kernel,
        out_shape=(jax.ShapeDtypeStruct((2048, 512), BF), jax.ShapeDtypeStruct((512, 2048), BF)),
        compiler_params=pltpu.CompilerParams(vmem_limit_bytes=12 << 20),
    )(place, jnp.asarray(nat.reshape(2048, 512)), jnp.asarray(natt))


def slot_waves(spec_ref, z, b, pid, leg):
    lane = lanes((32, 128))
    sp = load_block(spec_ref, z, b)
    mask = even_mask((16, RP), pid)
    even = jnp.where(mask, sp, 0.0).astype(BF)
    odd = jnp.where(mask, 0.0, sp).astype(BF)
    wide = jnp.concatenate([even, odd] * 4, axis=0)
    p = lax.dot_general(leg, wide, (((1,), (1,)), ((), ())), preferred_element_type=F32)
    return jnp.where(lane < 32, p[0:32], jnp.where(lane < 64, p[32:64], jnp.where(lane < 96, p[64:96], p[96:128])))


def combine_kernel(at_ref, leg_ref, got_ref, both_ref):
    core = at_ref[2]
    lane = lanes((64, 128))
    for b in range(2):
        for ref, half in ((leg_ref, core), (got_ref, 1 - core)):
            at = pl.ds(pl.multiple_of(half * 64, 64), 64)
            both_ref[b, at, 0:1024] = ref[b, :, 0:1024]
            col = jnp.broadcast_to(ref[b, :, 1024:R].astype(F32), (64, 128))
            both_ref[b, at, 1024:RP] = jnp.where(lane == 0, col, 0.0).astype(BF)


def combine(at, leg, got):
    return pl.pallas_call(
        combine_kernel,
        grid_spec=pltpu.PrefetchScalarGridSpec(
            num_scalar_prefetch=1,
            grid=(8,),
            in_specs=[pl.BlockSpec((2, 64, R), lambda i, at: (2 * i + at[2], 0, 0))] * 2,
            out_specs=pl.BlockSpec((2, 128, RP), lambda i, at: (i, 0, 0)),
        ),
        out_shape=jax.ShapeDtypeStruct((16, 128, RP), BF),
        compiler_params=pltpu.CompilerParams(vmem_limit_bytes=8 << 20),
    )(at, leg, got)


def inverse_kernel(first, pid_ref, at_ref, spec_ref, leg_ref, *refs):
    if first:
        var_ref, gauss_ref, out_ref, acc_ref = refs
        acc_ref[:, 16:32, :] = jnp.zeros((32, 16, 128), F32)
        gauss = jnp.broadcast_to(gauss_ref[...], (64, 64))
        gauss = jnp.sum(jnp.where(rows((64, 64)) == lanes((64, 64)), gauss, 0.0), axis=1, keepdims=True)
        rest = var_ref[...] * gauss
        for n in range(3):
            term = rest.astype(BF).astype(F32)
            rest = rest - term
            for jh in range(2):
                acc_ref[:, 16 + 2 * n + jh, :] = term[32 * jh : 32 * jh + 32, :]
    else:
        out_ref, acc_ref = refs
        tile = spec_ref[0, 256:272, :].astype(F32)
        for z in range(1, 8):
            tile = tile + spec_ref[z, 256:272, :].astype(F32)
        tile = split_tile(join_tile(tile)).astype(BF)
        out_ref[:, 16:32, :] = jnp.broadcast_to(tile[None], (32, 16, 128))
    for t in range(16):
        pid = pid_ref[at_ref[0] + 4 * (t // 2) + t % 2]
        acc_ref[:, t, :] = slot_waves(spec_ref, t // 2, t % 2, pid, leg_ref[t])
    if first:
        out_ref[...] = acc_ref[...].astype(BF)
    else:
        out_ref[:, 0:16, :] = acc_ref[...].astype(BF)


def legendre_inverse(pids, at, spec, leg, *extra):
    first = len(extra) > 0
    return pl.pallas_call(
        functools.partial(inverse_kernel, first),
        in_specs=[SMEM, SMEM] + [VMEM] * (2 + len(extra)),
        out_shape=jax.ShapeDtypeStruct((32, 32, 128), BF),
        scratch_shapes=[pltpu.VMEM((32, 32 if first else 16, 128), F32)],
        compiler_params=pltpu.CompilerParams(vmem_limit_bytes=12 << 20),
    )(pids, at, spec, leg, *extra)


def arrange_variance(x_ref, b):
    row, lane = rows((128, 128)), lanes((128, 128))
    keep = jnp.where(row == lane, 1.0, 0.0).astype(BF)
    turn = jnp.where(row + lane == 127, 1.0, 0.0).astype(BF)
    er, el = rows((32, 128)), lanes((32, 128))
    used = (lax.rem(er, 16) < 6) & (lax.rem(el, 32) // 8 == 2 * (er // 16) + lax.rem(er, 2))
    total = None
    for q, (a, order) in enumerate(((b, keep), (7 - b, turn), (8 + b, keep), (15 - b, turn))):
        terms = jnp.concatenate([x_ref[2 * a, 16:32, :], x_ref[2 * a + 1, 16:32, :]], axis=0)
        down = lax.dot_general(order, terms, (((1,), (1,)), ((), ())), preferred_element_type=F32).astype(BF)
        spread = jnp.where(used & (el // 32 == q), 1.0, 0.0).astype(BF)
        part = jnp.dot(down, spread, preferred_element_type=F32)
        total = part if total is None else total + part
    return total


def grid_kernel(first, x_ref, fold_ref, tt_ref, t_ref, *refs):
    x = x_ref[:, 0:16, :].reshape(512, 128)
    if first:
        y_ref, var_ref, hat_ref = refs
        for b in range(4):
            var_ref[128 * b : 128 * b + 128, :] = arrange_variance(x_ref, b)
    else:
        var_ref, y_ref, hat_ref = refs
        tile = jnp.sum(x_ref[:, 16:32, :].astype(F32), axis=0)
        gram = pltpu.roll(join_tile(tile), 120, 1)
        mix = tile_of(splat_factor(gram)[1], True, K)
        mix = jnp.concatenate([mix] * 16, axis=0)
    for g in range(4):
        f = fold_ref[:, 128 * g : 128 * g + 128].astype(F32)
        if first:
            f = jnp.where(lax.rem(rows((128, 128)), 8) == lax.rem(lanes((128, 128)), 8), f, 0.0)
            hat = jnp.dot(x, f.astype(BF), preferred_element_type=F32)
        else:
            f = f * mix
            hi = f.astype(BF)
            low = (f - hi.astype(F32)).astype(BF)
            hat = jnp.dot(x, hi, preferred_element_type=F32) + jnp.dot(x, low, preferred_element_type=F32)
        hat_ref[512 * g : 512 * g + 512, :] = hat.astype(BF)
    grid = jnp.dot(tt_ref[...], hat_ref[...], preferred_element_type=F32)
    scaled = (grid * var_ref[...]).astype(BF)
    lane = lanes((1, 128))
    out = None
    for g in range(4):
        part = jnp.dot(t_ref[512 * g : 512 * g + 512, :], scaled, preferred_element_type=F32)
        sign = jnp.ones((1, 128), F32)
        for q in range(4):
            if SIGNS[g, q] < 0:
                sign = jnp.where((lane >= 32 * q) & (lane < 32 * q + 32), -1.0, sign)
        part = part * sign
        part = part + pltpu.roll(part, 64, 1)
        part = part + pltpu.roll(part, 32, 1)
        out = part if out is None else jnp.where(lane >= 32 * g, part, out)
    y_ref[...] = out.astype(BF).reshape(32, 16, 128)


def grid_stage(x, fold, tt, t, var):
    first = var is None
    y = jax.ShapeDtypeStruct((32, 16, 128), BF)
    return pl.pallas_call(
        functools.partial(grid_kernel, first),
        out_shape=(y, jax.ShapeDtypeStruct((512, 128), F32)) if first else y,
        scratch_shapes=[pltpu.VMEM((2048, 128), BF)],
        compiler_params=pltpu.CompilerParams(vmem_limit_bytes=12 << 20),
    )(*((x, fold, tt, t) if first else (x, fold, tt, t, var)))


def forward_kernel(pid_ref, at_ref, y_ref, leg_ref, out_ref, wide_ref):
    wide_ref[...] = y_ref[...].astype(F32)
    lane = lanes((32, 128))
    for b in range(4):
        zt = jnp.concatenate([wide_ref[:, 4 * b + s, :] for s in range(4)], axis=0).T
        blocks = [
            jnp.concatenate([zt[32 * g + 8 * jj : 32 * g + 8 * jj + 8, :] for g in range(4)], axis=0)
            for jj in range(4)
        ]
        done = []
        for s in range(4):
            t = 4 * b + s
            lhs = None
            for jj in range(4):
                shift = (32 * (jj - s)) % 128
                v = pltpu.roll(blocks[jj], shift, 1) if shift else blocks[jj]
                lhs = v if lhs is None else jnp.where(lane >= 32 * jj, v, lhs)
            p = jnp.dot(lhs.astype(BF), leg_ref[t], preferred_element_type=F32)
            mask = even_mask((16, RP), pid_ref[at_ref[0] + 4 * (t // 2) + t % 2])
            done.append(jnp.where(mask, p[0:16], p[16:32]))
        for u in range(2):
            for n, v in enumerate(pack(done[2 * u : 2 * u + 2], jnp.zeros((16, 128), F32))):
                out_ref[2 * b + u, 16 * n : 16 * n + 16, :] = v


def legendre_forward(pids, at, y, leg):
    return pl.pallas_call(
        forward_kernel,
        in_specs=[SMEM, SMEM, VMEM, VMEM],
        out_shape=jax.ShapeDtypeStruct((8, 272, 128), BF),
        scratch_shapes=[pltpu.VMEM((32, 16, 128), F32)],
        compiler_params=pltpu.CompilerParams(vmem_limit_bytes=12 << 20),
    )(pids, at, y, leg)


def gram_tile(blocks):
    sh = jnp.concatenate(blocks, axis=0)
    hi = sh.astype(BF)
    low = (sh - hi.astype(F32)).astype(BF)
    both = jnp.concatenate([hi, low, jnp.zeros((64, RP), BF)], axis=0)
    full = lax.dot_general(both[0:64], both, (((1,), (1,)), ((), ())), preferred_element_type=F32)
    total = None
    for a in range(2):
        for b in range(2):
            for i in range(4):
                v = full[32 * a + 8 * i : 32 * a + 8 * i + 8, :]
                shift = (128 - (32 * b + 8 * i)) % 128
                v = pltpu.roll(v, shift, 1) if shift else v
                total = v if total is None else total + v
    return jnp.where(lanes((8, 128)) < 8, total, 0.0)


def summed_blocks(parts_ref, table_ref):
    out = []
    for b in range(2):
        total = load_block(parts_ref, 0, b)
        for z in range(1, parts_ref.shape[0]):
            total = total + load_block(parts_ref, z, b)
        out.append(total * table_ref[b : b + 1, :])
    return out


def owner_kernel(parts_ref, table_ref, out_ref):
    sh = summed_blocks(parts_ref, table_ref)
    tile = split_tile(pltpu.roll(gram_tile(sh), 8, 1))
    tile = jnp.concatenate([tile, jnp.zeros((8, 128), F32)], axis=0)
    pieces = pack([sh[b] * table_ref[2 + b : 3 + b, :] for b in range(2)], tile)
    for z in range(out_ref.shape[0]):
        for n, v in enumerate(pieces):
            out_ref[z, 16 * n : 16 * n + 16, :] = v


def owner_step(parts, table):
    return pl.pallas_call(
        owner_kernel,
        out_shape=jax.ShapeDtypeStruct((8, 272, 128), BF),
        compiler_params=pltpu.CompilerParams(vmem_limit_bytes=12 << 20),
    )(parts, table)


def last_kernel(parts_ref, table_ref, sh_ref, gram_ref):
    sh = summed_blocks(parts_ref, table_ref)
    for b in range(2):
        sh_ref[16 * b : 16 * b + 16, :] = sh[b]
    tile = gram_tile(sh)
    line = tile[0:1, :]
    for i in range(1, K):
        line = line + pltpu.roll(tile[i : i + 1, :], 8 * i, 1)
    gram_ref[...] = jnp.broadcast_to(line, gram_ref.shape)


def last_step(parts, table):
    return pl.pallas_call(
        last_kernel,
        out_shape=(jax.ShapeDtypeStruct((32, RP), F32), jax.ShapeDtypeStruct((128, 128), F32)),
        compiler_params=pltpu.CompilerParams(vmem_limit_bytes=12 << 20),
    )(parts, table)


def finish_kernel(sh_ref, gram_ref, other_ref, table_ref, modes_ref, lower_ref):
    line = jnp.sum(gram_ref[...] + other_ref[...], axis=0, keepdims=True)
    row = rows((8, 128))
    gram = jnp.broadcast_to(line, (8, 128))
    for i in range(1, K):
        gram = jnp.where(row == i, jnp.broadcast_to(pltpu.roll(line, 128 - 8 * i, 1), (8, 128)), gram)
    low, inv = splat_factor(gram)
    lower_ref[...] = tile_of(low, False, 0)
    coefs = []
    for q in range(K):
        coef = jnp.zeros((8, 128), F32)
        for i in range(q, K):
            coef = jnp.where(row == i, inv[i][q], coef)
        coefs.append(jnp.concatenate([coef] * (RP // 128), axis=1))
    for b in range(2):
        cos, sin = table_ref[4 + b : 5 + b, :], table_ref[6 + b : 7 + b, :]
        parts = []
        for c in range(2):
            block = sh_ref[16 * b + 8 * c : 16 * b + 8 * c + 8, :]
            out = coefs[0] * block[0:1, :]
            for q in range(1, K):
                out = out + coefs[q] * block[q : q + 1, :]
            parts.append(out)
        for c, v in enumerate((cos * parts[0] + sin * parts[1], sin * parts[0] - cos * parts[1])):
            modes_ref[b, :, c, 0:1024] = v[:, 0:1024]
            modes_ref[b, :, c, 1024:R] = v[:, 1024:R]


def finish(sh, grams, others, table):
    return pl.pallas_call(
        finish_kernel,
        out_shape=(jax.ShapeDtypeStruct((2, K, 2, R), F32), jax.ShapeDtypeStruct((8, 128), F32)),
        compiler_params=pltpu.CompilerParams(vmem_limit_bytes=12 << 20),
    )(sh, grams, others, table)


def body(start_block, legendre, variance, gauss_weight, pair_of_slot):
    lat, zpos, core = lax.axis_index("lat"), lax.axis_index("z"), lax.axis_index("c")
    at = jnp.stack([lat * 32 + core * 2, zpos * 4, core]).astype(jnp.int32)
    got = lax.ppermute(legendre, "c", [(0, 1), (1, 0)])
    spec, table = start_step(pair_of_slot, at, start_block)
    spec = lax.all_to_all(spec, "z", 0, 0, tiled=True)

    both = combine(at, legendre, got)
    pids = pair_of_slot.reshape(16, 8, 2, 2).transpose(0, 2, 1, 3).reshape(1, 512)
    place = jnp.where(pids % 2 == 0, pids, T_SIZE - pids) // 2
    t, tt = slot_tables(place)
    spec, both, t, tt = lax.optimization_barrier((spec, both, t, tt))
    fold = jnp.asarray(fold_matrix(), BF)

    for step in range(STEPS):
        if step == 0:
            x = legendre_inverse(pair_of_slot, at, spec, both, variance, gauss_weight.reshape(1, 64))
        else:
            spec = lax.all_to_all(spec, "z", 0, 0, tiled=True)
            x = legendre_inverse(pair_of_slot, at, spec, both)
        x = lax.all_to_all(x, ("lat", "c"), 0, 0, tiled=True)
        if step == 0:
            y, var = grid_stage(x, fold, tt, t, None)
        else:
            y = grid_stage(x, fold, tt, t, var)
        y = lax.all_to_all(y, ("lat", "c"), 0, 0, tiled=True)
        parts = legendre_forward(pair_of_slot, at, y, both)
        parts = lax.all_to_all(parts, "z", 0, 0, tiled=True)
        if step + 1 < STEPS:
            spec = owner_step(parts, table)
    sh, gram = last_step(parts, table)
    grams = lax.all_to_all(gram.reshape(128, 1, 128), ("lat", "z"), 0, 0, tiled=True).reshape(128, 128)
    others = lax.ppermute(grams, "c", [(0, 1), (1, 0)])
    modes, lower = finish(sh, grams, others, table)
    return modes, lower[:, :K]


def solution(mesh):
    fine = Mesh(mesh.devices.reshape(16, 8, 2), ("lat", "z", "c"))
    placed = (
        P(("lat", "z", "c"), None, None, None),
        P("lat", ("z", "c"), None),
        P(("z", "c"), "lat"),
        P(("z", "c")),
        P(),
    )
    return jax.shard_map(
        body,
        mesh=fine,
        in_specs=placed,
        out_specs=(P(("lat", "z", "c"), None, None, None), P()),
        check_vma=False,
    )
```

```python
import functools
import math

import jax
import jax.numpy as jnp
import numpy as np
from jax import lax
from jax.experimental import pallas as pl
from jax.experimental.pallas import tpu as pltpu
from jax.sharding import Mesh
from jax.sharding import PartitionSpec as P

T_SIZE = 1023
NLON = 2048
K = 8
STEPS = 3
NPAIR = 512
R = 1025
RP = 1152
BF = jnp.bfloat16
F32 = jnp.float32
GSCALE = 1.0 / (2.0 * NPAIR * R)
SIGNS = np.array([[1, 1, 1, 1], [1, -1, 1, -1], [1, -1, -1, 1], [1, 1, -1, -1]], np.float32)


def natural_tables():
    q = np.arange(512)[:, None]
    i2 = 2 * np.arange(256)[None, :] + 1
    out = []
    for m in (2 * q, 1023 - 2 * q):
        angle = (m * i2 % 4096) * (2.0 * math.pi / 4096)
        out += [np.cos(angle), np.sin(angle)]
    return np.stack(out).astype(jnp.bfloat16)


def fold_matrix():
    f = np.zeros((4, 4, K, 4, 4, 4, K), np.float32)
    for jj in range(4):
        for g in range(4):
            for q in range(4):
                f[jj, g, :, g, q, jj, :] = SIGNS[g, q]
    return f.reshape(128, 512)


def lanes(shape):
    return lax.broadcasted_iota(jnp.int32, shape, len(shape) - 1)


def rows(shape):
    return lax.broadcasted_iota(jnp.int32, shape, len(shape) - 2)


def split_tile(g):
    hi = g.astype(BF).astype(F32)
    rest = g - hi
    mid = rest.astype(BF).astype(F32)
    low = (rest - mid).astype(BF).astype(F32)
    return hi + pltpu.roll(mid, 8, 1) + pltpu.roll(low, 16, 1)


def join_tile(t):
    g = t + pltpu.roll(t, 120, 1) + pltpu.roll(t, 112, 1)
    lane = lanes(t.shape)
    return jnp.where((lane >= 8) & (lane < 16) & (rows(t.shape) < 8), g, 0.0)


def splat_factor(gram):
    g = [[jnp.broadcast_to(gram[i : i + 1, j : j + 1] * GSCALE, (8, 128)) for j in range(i + 1)] for i in range(K)]
    low = [[None] * K for _ in range(K)]
    inv = [[None] * K for _ in range(K)]
    for j in range(K):
        d = g[j][j]
        for p in range(j):
            d = d - low[j][p] * low[j][p]
        r = lax.rsqrt(d)
        r = r * (1.5 - 0.5 * d * r * r)
        low[j][j] = d * r
        inv[j][j] = r
        for i in range(j + 1, K):
            v = g[i][j]
            for p in range(j):
                v = v - low[i][p] * low[j][p]
            low[i][j] = v * r
    for j in range(K):
        for i in range(j + 1, K):
            v = low[i][j] * inv[j][j]
            for p in range(j + 1, i):
                v = v + low[i][p] * inv[p][j]
            inv[i][j] = -(v * inv[i][i])
    return low, inv


def tile_of(entries, transposed, period):
    row, lane = rows((8, 128)), lanes((8, 128))
    if period:
        lane = lax.rem(lane, period)
    out = jnp.zeros((8, 128), F32)
    for i in range(K):
        for j in range(i + 1):
            r, l = (j, i) if transposed else (i, j)
            out = jnp.where((row == r) & (lane == l), entries[i][j], out)
    return out


def even_mask(shape, pid):
    first = (lanes(shape) < T_SIZE + 1 - pid).astype(jnp.int32)
    return first != lax.rem(pid, 2)


def load_block(ref, z, b):
    main = [ref[z, (b * 8 + l) * 16 : (b * 8 + l) * 16 + 16, :].astype(F32) for l in range(8)]
    extra = ref[z, 256:264, :].astype(F32)
    last = [pltpu.roll(extra, 128 - n, 1) if n else extra for n in (2 * b, 2 * b + 1)]
    last = jnp.concatenate(last, axis=0)
    return jnp.concatenate(main + [jnp.where(lanes((16, 128)) == 0, last, 0.0)], axis=1)


def pack(blocks, tile):
    lane = lanes((8, 128))
    pieces = [v[:, 128 * l : 128 * l + 128].astype(BF) for v in blocks for l in range(8)]
    for n in range(4):
        col = blocks[n // 2][8 * (n % 2) : 8 * (n % 2) + 8, 1024:RP]
        tile = jnp.where(lane == n, pltpu.roll(col, n, 1) if n else col, tile)
    return pieces + [tile.astype(BF)]


def put(out_ref, z, pieces):
    for n, v in enumerate(pieces):
        out_ref[z, 16 * n : 16 * n + v.shape[0], :] = v


def start_kernel(pid_ref, at_ref, start_ref, out_ref, table_ref):
    base = at_ref[0] + at_ref[1]
    place, row = lanes((2, RP)), rows((2, RP))
    pid = jnp.where(row == 0, pid_ref[base], pid_ref[base + 1])
    first = place < T_SIZE + 1 - pid
    degree = jnp.where(first, pid + place, place - 1)
    wave = jnp.where(first, pid, T_SIZE - pid)
    level = degree.astype(F32)
    scale = lax.rsqrt(1.0 + level * (level + 1.0) * (4.0 / (T_SIZE * T_SIZE)))
    scale = jnp.where(place < R, scale * (1.0 / NLON), 0.0)
    weight = jnp.where(wave == 0, 1.0, 2.0).astype(F32)
    phase = wave.astype(F32) * (2.0 * math.pi / (2 * NLON))
    cos, sin = jnp.cos(phase), jnp.sin(phase)
    table_ref[0:2, :] = scale
    table_ref[2:4, :] = weight
    table_ref[4:6, :] = cos
    table_ref[6:8, :] = sin
    lane = lanes((8, 128))
    blocks = []
    for b in range(2):
        half = []
        for c in range(2):
            col = jnp.broadcast_to(start_ref[b, :, c, 1024:R], (8, 128))
            half.append(jnp.concatenate([start_ref[b, :, c, 0:1024], jnp.where(lane == 0, col, 0.0)], axis=1))
        re, im = half
        cb, sb, wb = cos[b : b + 1], sin[b : b + 1], weight[b : b + 1]
        blocks.append(jnp.concatenate([wb * (re * cb + im * sb), wb * (re * sb - im * cb)], axis=0))
    pieces = pack(blocks, jnp.zeros((8, 128), F32))
    for z in range(out_ref.shape[0]):
        put(out_ref, z, pieces)


SMEM = pl.BlockSpec(memory_space=pltpu.SMEM)
VMEM = pl.BlockSpec(memory_space=pltpu.VMEM)
HBM = pl.BlockSpec(memory_space=pltpu.HBM)


def start_step(pids, at, start):
    return pl.pallas_call(
        start_kernel,
        in_specs=[SMEM, SMEM, VMEM],
        out_shape=(jax.ShapeDtypeStruct((8, 264, 128), BF), jax.ShapeDtypeStruct((8, RP), F32)),
        compiler_params=pltpu.CompilerParams(vmem_limit_bytes=12 << 20),
    )(pids, at, start)


def table_kernel(place_ref, nat_ref, natt_ref, t_ref, tt_ref, sign_ref):
    hot = jnp.where(rows((512, 512)) == place_ref[...], 1.0, 0.0)
    hot_s = hot.T.astype(BF)
    hot = hot.astype(BF)
    for g in range(4):
        t_ref[512 * g : 512 * g + 512, :] = jnp.dot(hot_s, nat_ref[512 * g : 512 * g + 512, :], preferred_element_type=F32).astype(BF)
        tt_ref[:, 512 * g : 512 * g + 512] = jnp.dot(natt_ref[:, 512 * g : 512 * g + 512], hot, preferred_element_type=F32).astype(BF)
    turn = jnp.where(lax.rem(rows((512, 128)), 2) == 0, 1.0, -1.0).astype(BF)
    sign_ref[...] = jnp.dot(hot_s, turn, preferred_element_type=F32)


def slot_tables(place):
    nat = natural_tables()
    natt = np.ascontiguousarray(nat.transpose(2, 0, 1)).reshape(256, 2048)
    return pl.pallas_call(
        table_kernel,
        out_shape=(
            jax.ShapeDtypeStruct((2048, 256), BF),
            jax.ShapeDtypeStruct((256, 2048), BF),
            jax.ShapeDtypeStruct((512, 128), F32),
        ),
        compiler_params=pltpu.CompilerParams(vmem_limit_bytes=12 << 20),
    )(place, jnp.asarray(nat.reshape(2048, 256)), jnp.asarray(natt))


def slot_waves(spec_ref, z, b, pid, leg):
    lane = lanes((32, 128))
    sp = load_block(spec_ref, z, b)
    mask = even_mask((16, RP), pid)
    even = jnp.where(mask, sp, 0.0).astype(BF)
    odd = jnp.where(mask, 0.0, sp).astype(BF)
    wide = jnp.concatenate([even, odd] * 4, axis=0)
    p = lax.dot_general(leg, wide, (((1,), (1,)), ((), ())), preferred_element_type=F32)
    return jnp.where(lane < 32, p[0:32], jnp.where(lane < 64, p[32:64], jnp.where(lane < 96, p[64:96], p[96:128])))


def combine_kernel(at_ref, leg_ref, got_ref, both_ref, sems):
    core = at_ref[2]
    copies = []
    for z in range(8):
        for n, (ref, half) in enumerate(((leg_ref, core), (got_ref, 1 - core))):
            copy = pltpu.make_async_copy(
                ref.at[pl.ds(4 * z + 2 * core, 2)],
                both_ref.at[pl.ds(2 * z, 2), pl.ds(pl.multiple_of(half * 64, 64), 64)],
                sems.at[2 * z + n],
            )
            copy.start()
            copies.append(copy)
    for copy in copies:
        copy.wait()


def combine(at, leg, got):
    return pl.pallas_call(
        combine_kernel,
        in_specs=[SMEM, HBM, HBM],
        out_specs=HBM,
        out_shape=jax.ShapeDtypeStruct((16, 128, R), BF),
        scratch_shapes=[pltpu.SemaphoreType.DMA((16,))],
        compiler_params=pltpu.CompilerParams(vmem_limit_bytes=8 << 20),
    )(at, leg, got)


def whole(leg_ref, t):
    last = jnp.broadcast_to(leg_ref[t, :, 1024:R].astype(F32), (128, 128))
    last = jnp.where(lanes((128, 128)) == 0, last, 0.0).astype(BF)
    return jnp.concatenate([leg_ref[t, :, 0:1024], last], axis=1)


def inverse_kernel(first, pid_ref, at_ref, spec_ref, leg_ref, *refs):
    if first:
        var_ref, gauss_ref, out_ref, acc_ref = refs
        acc_ref[:, 16:24, :] = jnp.zeros((32, 8, 128), F32)
        gauss = jnp.broadcast_to(gauss_ref[...], (64, 64))
        gauss = jnp.sum(jnp.where(rows((64, 64)) == lanes((64, 64)), gauss, 0.0), axis=1, keepdims=True)
        rest = var_ref[...] * gauss
        for n in range(3):
            term = rest.astype(BF).astype(F32)
            rest = rest - term
            for jh in range(2):
                acc_ref[:, 16 + 2 * n + jh, :] = term[32 * jh : 32 * jh + 32, :]
    else:
        out_ref, acc_ref = refs
        tile = spec_ref[0, 256:264, :].astype(F32)
        for z in range(1, 8):
            tile = tile + spec_ref[z, 256:264, :].astype(F32)
        tile = split_tile(join_tile(tile)).astype(BF)
        out_ref[:, 16:24, :] = jnp.broadcast_to(tile[None], (32, 8, 128))
    for t in range(16):
        pid = pid_ref[at_ref[0] + 4 * (t // 2) + t % 2]
        acc_ref[:, t, :] = slot_waves(spec_ref, t // 2, t % 2, pid, whole(leg_ref, t))
    if first:
        out_ref[...] = acc_ref[...].astype(BF)
    else:
        out_ref[:, 0:16, :] = acc_ref[...].astype(BF)


def legendre_inverse(pids, at, spec, leg, *extra):
    first = len(extra) > 0
    return pl.pallas_call(
        functools.partial(inverse_kernel, first),
        in_specs=[SMEM, SMEM] + [VMEM] * (2 + len(extra)),
        out_shape=jax.ShapeDtypeStruct((32, 24, 128), BF),
        scratch_shapes=[pltpu.VMEM((32, 24 if first else 16, 128), F32)],
        compiler_params=pltpu.CompilerParams(vmem_limit_bytes=12 << 20),
    )(pids, at, spec, leg, *extra)


def arrange_variance(x_ref, b):
    row, lane = rows((128, 128)), lanes((128, 128))
    keep = jnp.where(row == lane, 1.0, 0.0).astype(BF)
    turn = jnp.where(row + lane == 127, 1.0, 0.0).astype(BF)
    er, el = rows((16, 128)), lanes((16, 128))
    used = (lax.rem(er, 8) < 6) & (lax.rem(el, 32) // 8 == 2 * (er // 8) + lax.rem(er, 2))
    halves = []
    for places in (
        ((b, keep), (7 - b, turn), (8 + b, keep), (15 - b, turn)),
        ((3 - b, turn), (4 + b, keep), (11 - b, turn), (12 + b, keep)),
    ):
        total = None
        for q, (a, order) in enumerate(places):
            terms = jnp.concatenate([x_ref[2 * a, 16:24, :], x_ref[2 * a + 1, 16:24, :]], axis=0)
            down = lax.dot_general(order, terms, (((1,), (1,)), ((), ())), preferred_element_type=F32).astype(BF)
            spread = jnp.where(used & (el // 32 == q), 1.0, 0.0).astype(BF)
            part = jnp.dot(down, spread, preferred_element_type=F32)
            total = part if total is None else total + part
        halves.append(total)
    return jnp.concatenate(halves, axis=1)


def grid_kernel(first, x_ref, fold_ref, tt_ref, t_ref, sign_ref, *refs):
    x = x_ref[:, 0:16, :].reshape(512, 128)
    if first:
        y_ref, var_ref, hat_ref = refs
        for b in range(2):
            var_ref[128 * b : 128 * b + 128, :] = arrange_variance(x_ref, b)
    else:
        var_ref, y_ref, hat_ref = refs
        tile = jnp.sum(x_ref[:, 16:24, :].astype(F32), axis=0)
        gram = pltpu.roll(join_tile(tile), 120, 1)
        mix = tile_of(splat_factor(gram)[1], True, K)
        mix = jnp.concatenate([mix] * 16, axis=0)
    sign = sign_ref[...]
    for g in range(4):
        f = fold_ref[:, 128 * g : 128 * g + 128].astype(F32)
        if first:
            f = jnp.where(lax.rem(rows((128, 128)), 8) == lax.rem(lanes((128, 128)), 8), f, 0.0)
            hat = jnp.dot(x, f.astype(BF), preferred_element_type=F32)
        else:
            f = f * mix
            hi = f.astype(BF)
            low = (f - hi.astype(F32)).astype(BF)
            hat = jnp.dot(x, hi, preferred_element_type=F32) + jnp.dot(x, low, preferred_element_type=F32)
        turned = hat * sign if g == 0 else hat * -sign
        to = (0, 1, 3, 2)[g]
        hat_ref[512 * g : 512 * g + 512, 0:128] = hat.astype(BF)
        hat_ref[512 * to : 512 * to + 512, 128:256] = turned.astype(BF)
    grid = jnp.dot(tt_ref[...], hat_ref[...], preferred_element_type=F32)
    scaled = (grid * var_ref[...]).astype(BF)
    lane = lanes((1, 128))
    parts = [jnp.dot(t_ref[512 * g : 512 * g + 512, :], scaled, preferred_element_type=F32) for g in range(4)]
    out = None
    for g in range(4):
        turned = parts[(0, 1, 3, 2)[g]][:, 128:256]
        part = parts[g][:, 0:128] + (turned * sign if g == 0 else turned * -sign)
        flip = jnp.ones((1, 128), F32)
        for q in range(4):
            if SIGNS[g, q] < 0:
                flip = jnp.where((lane >= 32 * q) & (lane < 32 * q + 32), -1.0, flip)
        part = part * flip
        part = part + pltpu.roll(part, 64, 1)
        part = part + pltpu.roll(part, 32, 1)
        out = part if out is None else jnp.where(lane >= 32 * g, part, out)
    y_ref[...] = out.astype(BF).reshape(32, 16, 128)


def grid_stage(x, fold, tt, t, sign, var):
    first = var is None
    y = jax.ShapeDtypeStruct((32, 16, 128), BF)
    return pl.pallas_call(
        functools.partial(grid_kernel, first),
        out_shape=(y, jax.ShapeDtypeStruct((256, 256), F32)) if first else y,
        scratch_shapes=[pltpu.VMEM((2048, 256), BF)],
        compiler_params=pltpu.CompilerParams(vmem_limit_bytes=12 << 20),
    )(*((x, fold, tt, t, sign) if first else (x, fold, tt, t, sign, var)))


def forward_kernel(pid_ref, at_ref, y_ref, leg_ref, out_ref, wide_ref):
    wide_ref[...] = y_ref[...].astype(F32)
    lane = lanes((32, 128))
    for b in range(4):
        zt = jnp.concatenate([wide_ref[:, 4 * b + s, :] for s in range(4)], axis=0).T
        blocks = [
            jnp.concatenate([zt[32 * g + 8 * jj : 32 * g + 8 * jj + 8, :] for g in range(4)], axis=0)
            for jj in range(4)
        ]
        done = []
        for s in range(4):
            t = 4 * b + s
            lhs = None
            for jj in range(4):
                shift = (32 * (jj - s)) % 128
                v = pltpu.roll(blocks[jj], shift, 1) if shift else blocks[jj]
                lhs = v if lhs is None else jnp.where(lane >= 32 * jj, v, lhs)
            p = jnp.dot(lhs.astype(BF), whole(leg_ref, t), preferred_element_type=F32)
            mask = even_mask((16, RP), pid_ref[at_ref[0] + 4 * (t // 2) + t % 2])
            done.append(jnp.where(mask, p[0:16], p[16:32]))
        for u in range(2):
            put(out_ref, 2 * b + u, pack(done[2 * u : 2 * u + 2], jnp.zeros((8, 128), F32)))


def legendre_forward(pids, at, y, leg):
    return pl.pallas_call(
        forward_kernel,
        in_specs=[SMEM, SMEM, VMEM, VMEM],
        out_shape=jax.ShapeDtypeStruct((8, 264, 128), BF),
        scratch_shapes=[pltpu.VMEM((32, 16, 128), F32)],
        compiler_params=pltpu.CompilerParams(vmem_limit_bytes=12 << 20),
    )(pids, at, y, leg)


def gram_tile(blocks):
    sh = jnp.concatenate(blocks, axis=0)
    hi = sh.astype(BF)
    low = (sh - hi.astype(F32)).astype(BF)
    both = jnp.concatenate([hi, low, jnp.zeros((64, RP), BF)], axis=0)
    full = lax.dot_general(both[0:64], both, (((1,), (1,)), ((), ())), preferred_element_type=F32)
    total = None
    for a in range(2):
        for b in range(2):
            for i in range(4):
                v = full[32 * a + 8 * i : 32 * a + 8 * i + 8, :]
                shift = (128 - (32 * b + 8 * i)) % 128
                v = pltpu.roll(v, shift, 1) if shift else v
                total = v if total is None else total + v
    return jnp.where(lanes((8, 128)) < 8, total, 0.0)


def summed_blocks(parts_ref, table_ref):
    out = []
    for b in range(2):
        total = load_block(parts_ref, 0, b)
        for z in range(1, parts_ref.shape[0]):
            total = total + load_block(parts_ref, z, b)
        out.append(total * table_ref[b : b + 1, :])
    return out


def owner_kernel(parts_ref, table_ref, out_ref):
    sh = summed_blocks(parts_ref, table_ref)
    tile = split_tile(pltpu.roll(gram_tile(sh), 8, 1))
    pieces = pack([sh[b] * table_ref[2 + b : 3 + b, :] for b in range(2)], tile)
    for z in range(out_ref.shape[0]):
        put(out_ref, z, pieces)


def owner_step(parts, table):
    return pl.pallas_call(
        owner_kernel,
        out_shape=jax.ShapeDtypeStruct((8, 264, 128), BF),
        compiler_params=pltpu.CompilerParams(vmem_limit_bytes=12 << 20),
    )(parts, table)


def last_kernel(parts_ref, table_ref, sh_ref, gram_ref):
    sh = summed_blocks(parts_ref, table_ref)
    for b in range(2):
        sh_ref[16 * b : 16 * b + 16, :] = sh[b]
    tile = gram_tile(sh)
    line = tile[0:1, :]
    for i in range(1, K):
        line = line + pltpu.roll(tile[i : i + 1, :], 8 * i, 1)
    gram_ref[...] = jnp.broadcast_to(line, gram_ref.shape)


def last_step(parts, table):
    return pl.pallas_call(
        last_kernel,
        out_shape=(jax.ShapeDtypeStruct((32, RP), F32), jax.ShapeDtypeStruct((128, 128), F32)),
        compiler_params=pltpu.CompilerParams(vmem_limit_bytes=12 << 20),
    )(parts, table)


def finish_kernel(sh_ref, gram_ref, other_ref, table_ref, modes_ref, lower_ref):
    line = jnp.sum(gram_ref[...] + other_ref[...], axis=0, keepdims=True)
    row = rows((8, 128))
    gram = jnp.broadcast_to(line, (8, 128))
    for i in range(1, K):
        gram = jnp.where(row == i, jnp.broadcast_to(pltpu.roll(line, 128 - 8 * i, 1), (8, 128)), gram)
    low, inv = splat_factor(gram)
    lower_ref[...] = tile_of(low, False, 0)
    coefs = []
    for q in range(K):
        coef = jnp.zeros((8, 128), F32)
        for i in range(q, K):
            coef = jnp.where(row == i, inv[i][q], coef)
        coefs.append(jnp.concatenate([coef] * (RP // 128), axis=1))
    for b in range(2):
        cos, sin = table_ref[4 + b : 5 + b, :], table_ref[6 + b : 7 + b, :]
        parts = []
        for c in range(2):
            block = sh_ref[16 * b + 8 * c : 16 * b + 8 * c + 8, :]
            out = coefs[0] * block[0:1, :]
            for q in range(1, K):
                out = out + coefs[q] * block[q : q + 1, :]
            parts.append(out)
        for c, v in enumerate((cos * parts[0] + sin * parts[1], sin * parts[0] - cos * parts[1])):
            modes_ref[b, :, c, 0:1024] = v[:, 0:1024]
            modes_ref[b, :, c, 1024:R] = v[:, 1024:R]


def finish(sh, grams, others, table):
    return pl.pallas_call(
        finish_kernel,
        out_shape=(jax.ShapeDtypeStruct((2, K, 2, R), F32), jax.ShapeDtypeStruct((8, 128), F32)),
        compiler_params=pltpu.CompilerParams(vmem_limit_bytes=12 << 20),
    )(sh, grams, others, table)


def body(start_block, legendre, variance, gauss_weight, pair_of_slot):
    lat, zpos, core = lax.axis_index("lat"), lax.axis_index("z"), lax.axis_index("c")
    at = jnp.stack([lat * 32 + core * 2, zpos * 4, core]).astype(jnp.int32)
    got = lax.ppermute(legendre, "c", [(0, 1), (1, 0)])
    spec, table = start_step(pair_of_slot, at, start_block)
    spec = lax.all_to_all(spec, "z", 0, 0, tiled=True)

    both = combine(at, legendre, got)
    pids = pair_of_slot.reshape(16, 8, 2, 2).transpose(0, 2, 1, 3).reshape(1, 512)
    place = jnp.where(pids % 2 == 0, pids, T_SIZE - pids) // 2
    t, tt, sign = slot_tables(place)
    spec, both, t, tt, sign = lax.optimization_barrier((spec, both, t, tt, sign))
    fold = jnp.asarray(fold_matrix(), BF)

    for step in range(STEPS):
        if step == 0:
            x = legendre_inverse(pair_of_slot, at, spec, both, variance, gauss_weight.reshape(1, 64))
        else:
            spec = lax.all_to_all(spec, "z", 0, 0, tiled=True)
            x = legendre_inverse(pair_of_slot, at, spec, both)
        x = lax.all_to_all(x, ("lat", "c"), 0, 0, tiled=True)
        if step == 0:
            y, var = grid_stage(x, fold, tt, t, sign, None)
        else:
            y = grid_stage(x, fold, tt, t, sign, var)
        y = lax.all_to_all(y, ("lat", "c"), 0, 0, tiled=True)
        parts = legendre_forward(pair_of_slot, at, y, both)
        parts = lax.all_to_all(parts, "z", 0, 0, tiled=True)
        if step + 1 < STEPS:
            spec = owner_step(parts, table)
    sh, gram = last_step(parts, table)
    grams = lax.all_to_all(gram.reshape(128, 1, 128), ("lat", "z"), 0, 0, tiled=True).reshape(128, 128)
    others = lax.ppermute(grams, "c", [(0, 1), (1, 0)])
    modes, lower = finish(sh, grams, others, table)
    return modes, lower[:, :K]


def solution(mesh):
    fine = Mesh(mesh.devices.reshape(16, 8, 2), ("lat", "z", "c"))
    placed = (
        P(("lat", "z", "c"), None, None, None),
        P("lat", ("z", "c"), None),
        P(("z", "c"), "lat"),
        P(("z", "c")),
        P(),
    )
    return jax.shard_map(
        body,
        mesh=fine,
        in_specs=placed,
        out_specs=(P(("lat", "z", "c"), None, None, None), P()),
        check_vma=False,
    )
```

```python
import functools
import math

import jax
import jax.numpy as jnp
import numpy as np
from jax import lax
from jax.experimental import pallas as pl
from jax.experimental.pallas import tpu as pltpu
from jax.sharding import Mesh
from jax.sharding import PartitionSpec as P

T_SIZE = 1023
NLON = 2048
K = 8
STEPS = 3
NPAIR = 512
R = 1025
RP = 1152
ORDER = [3 * i % 8 for i in range(8)]
PLACE = [ORDER.index(i) for i in range(8)]
BF = jnp.bfloat16
F32 = jnp.float32
GSCALE = 1.0 / (2.0 * NPAIR * R)
SIGNS = np.array([[1, 1, 1, 1], [1, -1, 1, -1], [1, -1, -1, 1], [1, 1, -1, -1]], np.float32)


def natural_tables():
    q = np.arange(512)[:, None]
    i2 = 2 * np.arange(256)[None, :] + 1
    out = []
    for m in (2 * q, 1023 - 2 * q):
        angle = (m * i2 % 4096) * (2.0 * math.pi / 4096)
        out += [np.cos(angle), np.sin(angle)]
    return np.stack(out).astype(jnp.bfloat16)


def fold_matrix():
    f = np.zeros((4, 4, K, 4, 4, 4, K), np.float32)
    for jj in range(4):
        for g in range(4):
            for q in range(4):
                f[jj, g, :, g, q, jj, :] = SIGNS[g, q]
    return f.reshape(128, 512)


def lanes(shape):
    return lax.broadcasted_iota(jnp.int32, shape, len(shape) - 1)


def rows(shape):
    return lax.broadcasted_iota(jnp.int32, shape, len(shape) - 2)


def split_tile(g):
    hi = g.astype(BF).astype(F32)
    rest = g - hi
    mid = rest.astype(BF).astype(F32)
    low = (rest - mid).astype(BF).astype(F32)
    return hi + pltpu.roll(mid, 8, 1) + pltpu.roll(low, 16, 1)


def join_tile(t):
    g = t + pltpu.roll(t, 120, 1) + pltpu.roll(t, 112, 1)
    lane = lanes(t.shape)
    return jnp.where((lane >= 8) & (lane < 16) & (rows(t.shape) < 8), g, 0.0)


def splat_factor(gram):
    g = [[jnp.broadcast_to(gram[i : i + 1, j : j + 1] * GSCALE, (8, 128)) for j in range(i + 1)] for i in range(K)]
    low = [[None] * K for _ in range(K)]
    inv = [[None] * K for _ in range(K)]
    for j in range(K):
        d = g[j][j]
        for p in range(j):
            d = d - low[j][p] * low[j][p]
        r = lax.rsqrt(d)
        r = r * (1.5 - 0.5 * d * r * r)
        low[j][j] = d * r
        inv[j][j] = r
        for i in range(j + 1, K):
            v = g[i][j]
            for p in range(j):
                v = v - low[i][p] * low[j][p]
            low[i][j] = v * r
    for j in range(K):
        for i in range(j + 1, K):
            v = low[i][j] * inv[j][j]
            for p in range(j + 1, i):
                v = v + low[i][p] * inv[p][j]
            inv[i][j] = -(v * inv[i][i])
    return low, inv


def tile_of(entries, transposed, period):
    row, lane = rows((8, 128)), lanes((8, 128))
    if period:
        lane = lax.rem(lane, period)
    out = jnp.zeros((8, 128), F32)
    for i in range(K):
        for j in range(i + 1):
            r, l = (j, i) if transposed else (i, j)
            out = jnp.where((row == r) & (lane == l), entries[i][j], out)
    return out


def even_mask(shape, pid):
    first = (lanes(shape) < T_SIZE + 1 - pid).astype(jnp.int32)
    return first != lax.rem(pid, 2)


def load_block(ref, z, b):
    main = [ref[z, (b * 8 + l) * 16 : (b * 8 + l) * 16 + 16, :].astype(F32) for l in range(8)]
    extra = ref[z, 256:264, :].astype(F32)
    last = [pltpu.roll(extra, 128 - n, 1) if n else extra for n in (2 * b, 2 * b + 1)]
    last = jnp.concatenate(last, axis=0)
    return jnp.concatenate(main + [jnp.where(lanes((16, 128)) == 0, last, 0.0)], axis=1)


def pack(blocks, tile):
    lane = lanes((8, 128))
    pieces = [v[:, 128 * l : 128 * l + 128].astype(BF) for v in blocks for l in range(8)]
    for n in range(4):
        col = blocks[n // 2][8 * (n % 2) : 8 * (n % 2) + 8, 1024:RP]
        tile = jnp.where(lane == n, pltpu.roll(col, n, 1) if n else col, tile)
    return pieces + [tile.astype(BF)]


def put(out_ref, z, pieces):
    for n, v in enumerate(pieces):
        out_ref[z, 16 * n : 16 * n + v.shape[0], :] = v


def start_kernel(at_ref, start_ref, out_ref, table_ref):
    place, row = lanes((2, RP)), rows((2, RP))
    pid = jnp.where(row == 0, at_ref[2], at_ref[3])
    first = place < T_SIZE + 1 - pid
    degree = jnp.where(first, pid + place, place - 1)
    wave = jnp.where(first, pid, T_SIZE - pid)
    level = degree.astype(F32)
    scale = lax.rsqrt(1.0 + level * (level + 1.0) * (4.0 / (T_SIZE * T_SIZE)))
    scale = jnp.where(place < R, scale * (1.0 / NLON), 0.0)
    weight = jnp.where(wave == 0, 1.0, 2.0).astype(F32)
    phase = wave.astype(F32) * (2.0 * math.pi / (2 * NLON))
    cos, sin = jnp.cos(phase), jnp.sin(phase)
    table_ref[0:2, :] = scale
    table_ref[2:4, :] = weight
    table_ref[4:6, :] = cos
    table_ref[6:8, :] = sin
    lane = lanes((8, 128))
    blocks = []
    for b in range(2):
        half = []
        for c in range(2):
            col = jnp.broadcast_to(start_ref[b, :, c, 1024:R], (8, 128))
            half.append(jnp.concatenate([start_ref[b, :, c, 0:1024], jnp.where(lane == 0, col, 0.0)], axis=1))
        re, im = half
        cb, sb, wb = cos[b : b + 1], sin[b : b + 1], weight[b : b + 1]
        blocks.append(jnp.concatenate([wb * (re * cb + im * sb), wb * (re * sb - im * cb)], axis=0))
    pieces = pack(blocks, jnp.zeros((8, 128), F32))
    for z in range(out_ref.shape[0]):
        put(out_ref, z, pieces)


SMEM = pl.BlockSpec(memory_space=pltpu.SMEM)
VMEM = pl.BlockSpec(memory_space=pltpu.VMEM)
HBM = pl.BlockSpec(memory_space=pltpu.HBM)


def start_step(at, start):
    return pl.pallas_call(
        start_kernel,
        in_specs=[SMEM, VMEM],
        out_shape=(jax.ShapeDtypeStruct((8, 264, 128), BF), jax.ShapeDtypeStruct((8, RP), F32)),
        compiler_params=pltpu.CompilerParams(vmem_limit_bytes=12 << 20),
    )(at, start)


def table_kernel(place_ref, nat_ref, natt_ref, t_ref, tt_ref, sign_ref):
    hot = jnp.where(rows((512, 512)) == place_ref[...], 1.0, 0.0)
    hot_s = hot.T.astype(BF)
    hot = hot.astype(BF)
    for g in range(4):
        t_ref[512 * g : 512 * g + 512, :] = jnp.dot(hot_s, nat_ref[512 * g : 512 * g + 512, :], preferred_element_type=F32).astype(BF)
        tt_ref[:, 512 * g : 512 * g + 512] = jnp.dot(natt_ref[:, 512 * g : 512 * g + 512], hot, preferred_element_type=F32).astype(BF)
    turn = jnp.where(lax.rem(rows((512, 128)), 2) == 0, 1.0, -1.0).astype(BF)
    sign_ref[...] = jnp.dot(hot_s, turn, preferred_element_type=F32)


def slot_tables(place):
    nat = natural_tables()
    natt = np.ascontiguousarray(nat.transpose(2, 0, 1)).reshape(256, 2048)
    return pl.pallas_call(
        table_kernel,
        out_shape=(
            jax.ShapeDtypeStruct((2048, 256), BF),
            jax.ShapeDtypeStruct((256, 2048), BF),
            jax.ShapeDtypeStruct((512, 128), F32),
        ),
        compiler_params=pltpu.CompilerParams(vmem_limit_bytes=12 << 20),
    )(place, jnp.asarray(nat.reshape(2048, 256)), jnp.asarray(natt))


def slot_waves(spec_ref, z, b, pid, leg_ref, t):
    lane = lanes((32, 128))

    def own(pieces):
        return jnp.where(lane < 32, pieces[0], jnp.where(lane < 64, pieces[1], jnp.where(lane < 96, pieces[2], pieces[3])))

    main = [spec_ref[z, (b * 8 + l) * 16 : (b * 8 + l) * 16 + 16, :].astype(F32) for l in range(8)]
    sp = jnp.concatenate(main, axis=1)
    mask = even_mask((16, 1024), pid)
    even = jnp.where(mask, sp, 0.0).astype(BF)
    odd = jnp.where(mask, 0.0, sp).astype(BF)
    wide = jnp.concatenate([even, odd] * 4, axis=0)
    p = lax.dot_general(leg_ref[t, :, 0:1024], wide, (((1,), (1,)), ((), ())), preferred_element_type=F32)
    extra = spec_ref[z, 256:264, :].astype(F32)
    lane8, row8 = lanes((8, 128)), rows((8, 128))
    here = (lax.rem(lane8, 8) == row8) & (lax.rem(lane8 // 16, 2) == 1 - lax.rem(pid, 2))
    line = jnp.zeros((8, 128), F32)
    for c in range(2):
        col = jnp.broadcast_to(extra[:, 2 * b + c : 2 * b + c + 1], (8, 128))
        line = jnp.where(here & (lax.rem(lane8 // 8, 2) == c), col, line)
    line = jnp.sum(line, axis=0, keepdims=True)
    last = own([jnp.broadcast_to(leg_ref[t, 32 * jj : 32 * jj + 32, 1024:R].astype(F32), (32, 128)) for jj in range(4)])
    return own([p[32 * jj : 32 * jj + 32] for jj in range(4)]) + last * line


def combine_kernel(at_ref, leg_ref, got_ref, both_ref, sems):
    core = at_ref[1]
    copies = []
    for z in range(8):
        for n, (ref, half) in enumerate(((leg_ref, core), (got_ref, 1 - core))):
            copy = pltpu.make_async_copy(
                ref.at[pl.ds(4 * z + 2 * core, 2)],
                both_ref.at[pl.ds(2 * z, 2), pl.ds(pl.multiple_of(half * 64, 64), 64)],
                sems.at[2 * z + n],
            )
            copy.start()
            copies.append(copy)
    for copy in copies:
        copy.wait()


def combine(at, leg, got):
    return pl.pallas_call(
        combine_kernel,
        in_specs=[SMEM, HBM, HBM],
        out_specs=HBM,
        out_shape=jax.ShapeDtypeStruct((16, 128, R), BF),
        scratch_shapes=[pltpu.SemaphoreType.DMA((16,))],
        compiler_params=pltpu.CompilerParams(vmem_limit_bytes=8 << 20),
    )(at, leg, got)


def whole(leg_ref, t):
    last = jnp.broadcast_to(leg_ref[t, :, 1024:R].astype(F32), (128, 128))
    last = jnp.where(lanes((128, 128)) == 0, last, 0.0).astype(BF)
    return jnp.concatenate([leg_ref[t, :, 0:1024], last], axis=1)


def inverse_kernel(first, pid_ref, at_ref, spec_ref, leg_ref, *refs):
    if first:
        var_ref, gauss_ref, out_ref, acc_ref = refs
        acc_ref[:, 16:24, :] = jnp.zeros((32, 8, 128), F32)
        gauss = jnp.broadcast_to(gauss_ref[...], (64, 64))
        gauss = jnp.sum(jnp.where(rows((64, 64)) == lanes((64, 64)), gauss, 0.0), axis=1, keepdims=True)
        rest = var_ref[...] * gauss
        for n in range(3):
            term = rest.astype(BF).astype(F32)
            rest = rest - term
            for jh in range(2):
                acc_ref[:, 16 + 2 * n + jh, :] = term[32 * jh : 32 * jh + 32, :]
    else:
        out_ref, acc_ref = refs
        tile = spec_ref[0, 256:264, :].astype(F32)
        for z in range(1, 8):
            tile = tile + spec_ref[z, 256:264, :].astype(F32)
        tile = split_tile(join_tile(tile)).astype(BF)
        out_ref[:, 16:24, :] = jnp.broadcast_to(tile[None], (32, 8, 128))
    for t in range(16):
        pid = pid_ref[at_ref[0] + 4 * (t // 2) + t % 2]
        acc_ref[:, t, :] = slot_waves(spec_ref, PLACE[t // 2], t % 2, pid, leg_ref, t)
    if first:
        out_ref[...] = acc_ref[...].astype(BF)
    else:
        out_ref[:, 0:16, :] = acc_ref[...].astype(BF)


def legendre_inverse(pids, at, spec, leg, *extra):
    first = len(extra) > 0
    return pl.pallas_call(
        functools.partial(inverse_kernel, first),
        in_specs=[SMEM, SMEM] + [VMEM] * (2 + len(extra)),
        out_shape=jax.ShapeDtypeStruct((32, 24, 128), BF),
        scratch_shapes=[pltpu.VMEM((32, 24 if first else 16, 128), F32)],
        compiler_params=pltpu.CompilerParams(vmem_limit_bytes=12 << 20),
    )(pids, at, spec, leg, *extra)


def arrange_variance(x_ref, b):
    row, lane = rows((128, 128)), lanes((128, 128))
    keep = jnp.where(row == lane, 1.0, 0.0).astype(BF)
    turn = jnp.where(row + lane == 127, 1.0, 0.0).astype(BF)
    er, el = rows((16, 128)), lanes((16, 128))
    used = (lax.rem(er, 8) < 6) & (lax.rem(el, 32) // 8 == 2 * (er // 8) + lax.rem(er, 2))
    halves = []
    for places in (
        ((b, keep), (7 - b, turn), (8 + b, keep), (15 - b, turn)),
        ((3 - b, turn), (4 + b, keep), (11 - b, turn), (12 + b, keep)),
    ):
        total = None
        for q, (a, order) in enumerate(places):
            terms = jnp.concatenate([x_ref[2 * a, 16:24, :], x_ref[2 * a + 1, 16:24, :]], axis=0)
            down = lax.dot_general(order, terms, (((1,), (1,)), ((), ())), preferred_element_type=F32).astype(BF)
            spread = jnp.where(used & (el // 32 == q), 1.0, 0.0).astype(BF)
            part = jnp.dot(down, spread, preferred_element_type=F32)
            total = part if total is None else total + part
        halves.append(total)
    return jnp.concatenate(halves, axis=1)


def grid_kernel(first, x_ref, fold_ref, tt_ref, t_ref, sign_ref, *refs):
    x = x_ref[:, 0:16, :].reshape(512, 128)
    if first:
        y_ref, var_ref, hat_ref = refs
        for b in range(2):
            var_ref[128 * b : 128 * b + 128, :] = arrange_variance(x_ref, b)
    else:
        var_ref, y_ref, hat_ref = refs
        tile = jnp.sum(x_ref[:, 16:24, :].astype(F32), axis=0)
        gram = pltpu.roll(join_tile(tile), 120, 1)
        mix = tile_of(splat_factor(gram)[1], True, K)
        mix = jnp.concatenate([mix] * 16, axis=0)
    sign = sign_ref[...]
    for g in range(4):
        f = fold_ref[:, 128 * g : 128 * g + 128].astype(F32)
        if first:
            f = jnp.where(lax.rem(rows((128, 128)), 8) == lax.rem(lanes((128, 128)), 8), f, 0.0)
            hat = jnp.dot(x, f.astype(BF), preferred_element_type=F32)
        else:
            f = f * mix
            hi = f.astype(BF)
            low = (f - hi.astype(F32)).astype(BF)
            hat = jnp.dot(x, hi, preferred_element_type=F32) + jnp.dot(x, low, preferred_element_type=F32)
        turned = hat * sign if g == 0 else hat * -sign
        to = (0, 1, 3, 2)[g]
        hat_ref[512 * g : 512 * g + 512, 0:128] = hat.astype(BF)
        hat_ref[512 * to : 512 * to + 512, 128:256] = turned.astype(BF)
    grid = jnp.dot(tt_ref[...], hat_ref[...], preferred_element_type=F32)
    scaled = (grid * var_ref[...]).astype(BF)
    lane = lanes((1, 128))
    parts = [jnp.dot(t_ref[512 * g : 512 * g + 512, :], scaled, preferred_element_type=F32) for g in range(4)]
    out = None
    for g in range(4):
        turned = parts[(0, 1, 3, 2)[g]][:, 128:256]
        part = parts[g][:, 0:128] + (turned * sign if g == 0 else turned * -sign)
        flip = jnp.ones((1, 128), F32)
        for q in range(4):
            if SIGNS[g, q] < 0:
                flip = jnp.where((lane >= 32 * q) & (lane < 32 * q + 32), -1.0, flip)
        part = part * flip
        part = part + pltpu.roll(part, 64, 1)
        part = part + pltpu.roll(part, 32, 1)
        out = part if out is None else jnp.where(lane >= 32 * g, part, out)
    y_ref[...] = out.astype(BF).reshape(32, 16, 128)


def grid_stage(x, fold, tt, t, sign, var):
    first = var is None
    y = jax.ShapeDtypeStruct((32, 16, 128), BF)
    return pl.pallas_call(
        functools.partial(grid_kernel, first),
        out_shape=(y, jax.ShapeDtypeStruct((256, 256), F32)) if first else y,
        scratch_shapes=[pltpu.VMEM((2048, 256), BF)],
        compiler_params=pltpu.CompilerParams(vmem_limit_bytes=12 << 20),
    )(*((x, fold, tt, t, sign) if first else (x, fold, tt, t, sign, var)))


def forward_kernel(pid_ref, at_ref, y_ref, leg_ref, out_ref, wide_ref):
    wide_ref[...] = y_ref[...].astype(F32)
    lane = lanes((32, 128))
    for b in range(4):
        zt = jnp.concatenate([wide_ref[:, 4 * b + s, :] for s in range(4)], axis=0).T
        blocks = [
            jnp.concatenate([zt[32 * g + 8 * jj : 32 * g + 8 * jj + 8, :] for g in range(4)], axis=0)
            for jj in range(4)
        ]
        done = []
        for s in range(4):
            t = 4 * b + s
            lhs = None
            for jj in range(4):
                shift = (32 * (jj - s)) % 128
                v = pltpu.roll(blocks[jj], shift, 1) if shift else blocks[jj]
                lhs = v if lhs is None else jnp.where(lane >= 32 * jj, v, lhs)
            p = jnp.dot(lhs.astype(BF), whole(leg_ref, t), preferred_element_type=F32)
            mask = even_mask((16, RP), pid_ref[at_ref[0] + 4 * (t // 2) + t % 2])
            done.append(jnp.where(mask, p[0:16], p[16:32]))
        for u in range(2):
            put(out_ref, PLACE[2 * b + u], pack(done[2 * u : 2 * u + 2], jnp.zeros((8, 128), F32)))


def legendre_forward(pids, at, y, leg):
    return pl.pallas_call(
        forward_kernel,
        in_specs=[SMEM, SMEM, VMEM, VMEM],
        out_shape=jax.ShapeDtypeStruct((8, 264, 128), BF),
        scratch_shapes=[pltpu.VMEM((32, 16, 128), F32)],
        compiler_params=pltpu.CompilerParams(vmem_limit_bytes=12 << 20),
    )(pids, at, y, leg)


def gram_tile(blocks):
    sh = jnp.concatenate(blocks, axis=0)
    hi = sh.astype(BF)
    low = (sh - hi.astype(F32)).astype(BF)
    both = jnp.concatenate([hi, low, jnp.zeros((64, RP), BF)], axis=0)
    full = lax.dot_general(both[0:64], both, (((1,), (1,)), ((), ())), preferred_element_type=F32)
    total = None
    for a in range(2):
        for b in range(2):
            for i in range(4):
                v = full[32 * a + 8 * i : 32 * a + 8 * i + 8, :]
                shift = (128 - (32 * b + 8 * i)) % 128
                v = pltpu.roll(v, shift, 1) if shift else v
                total = v if total is None else total + v
    return jnp.where(lanes((8, 128)) < 8, total, 0.0)


def summed_blocks(parts_ref, table_ref):
    out = []
    for b in range(2):
        total = load_block(parts_ref, 0, b)
        for z in range(1, parts_ref.shape[0]):
            total = total + load_block(parts_ref, z, b)
        out.append(total * table_ref[b : b + 1, :])
    return out


def owner_kernel(parts_ref, table_ref, out_ref):
    sh = summed_blocks(parts_ref, table_ref)
    tile = split_tile(pltpu.roll(gram_tile(sh), 8, 1))
    pieces = pack([sh[b] * table_ref[2 + b : 3 + b, :] for b in range(2)], tile)
    for z in range(out_ref.shape[0]):
        put(out_ref, z, pieces)


def owner_step(parts, table):
    return pl.pallas_call(
        owner_kernel,
        out_shape=jax.ShapeDtypeStruct((8, 264, 128), BF),
        compiler_params=pltpu.CompilerParams(vmem_limit_bytes=12 << 20),
    )(parts, table)


def last_kernel(parts_ref, table_ref, sh_ref, gram_ref):
    sh = summed_blocks(parts_ref, table_ref)
    for b in range(2):
        sh_ref[16 * b : 16 * b + 16, :] = sh[b]
    tile = gram_tile(sh)
    line = tile[0:1, :]
    for i in range(1, K):
        line = line + pltpu.roll(tile[i : i + 1, :], 8 * i, 1)
    gram_ref[...] = jnp.broadcast_to(line, gram_ref.shape)


def last_step(parts, table):
    return pl.pallas_call(
        last_kernel,
        out_shape=(jax.ShapeDtypeStruct((32, RP), F32), jax.ShapeDtypeStruct((128, 128), F32)),
        compiler_params=pltpu.CompilerParams(vmem_limit_bytes=12 << 20),
    )(parts, table)


def finish_kernel(sh_ref, gram_ref, other_ref, table_ref, modes_ref, lower_ref):
    line = jnp.sum(gram_ref[...] + other_ref[...], axis=0, keepdims=True)
    row = rows((8, 128))
    gram = jnp.broadcast_to(line, (8, 128))
    for i in range(1, K):
        gram = jnp.where(row == i, jnp.broadcast_to(pltpu.roll(line, 128 - 8 * i, 1), (8, 128)), gram)
    low, inv = splat_factor(gram)
    lower_ref[...] = tile_of(low, False, 0)
    coefs = []
    for q in range(K):
        coef = jnp.zeros((8, 128), F32)
        for i in range(q, K):
            coef = jnp.where(row == i, inv[i][q], coef)
        coefs.append(jnp.concatenate([coef] * (RP // 128), axis=1))
    for b in range(2):
        cos, sin = table_ref[4 + b : 5 + b, :], table_ref[6 + b : 7 + b, :]
        parts = []
        for c in range(2):
            block = sh_ref[16 * b + 8 * c : 16 * b + 8 * c + 8, :]
            out = coefs[0] * block[0:1, :]
            for q in range(1, K):
                out = out + coefs[q] * block[q : q + 1, :]
            parts.append(out)
        for c, v in enumerate((cos * parts[0] + sin * parts[1], sin * parts[0] - cos * parts[1])):
            modes_ref[b, :, c, 0:1024] = v[:, 0:1024]
            modes_ref[b, :, c, 1024:R] = v[:, 1024:R]


def finish(sh, grams, others, table):
    return pl.pallas_call(
        finish_kernel,
        out_shape=(jax.ShapeDtypeStruct((2, K, 2, R), F32), jax.ShapeDtypeStruct((8, 128), F32)),
        compiler_params=pltpu.CompilerParams(vmem_limit_bytes=12 << 20),
    )(sh, grams, others, table)


def body(start_block, legendre, variance, gauss_weight, pair_of_slot):
    lat, zpos, core = lax.axis_index("lat"), lax.axis_index("z"), lax.axis_index("c")
    base = lat * 32 + core * 2
    own = lax.dynamic_slice(pair_of_slot, (base + zpos * 4,), (2,))
    at = jnp.concatenate([jnp.stack([base, core]).astype(jnp.int32), own])
    got = lax.ppermute(legendre, "c", [(0, 1), (1, 0)])
    spec, table = start_step(at, start_block)
    spec = lax.all_to_all(spec, "z", 0, 0, axis_index_groups=[ORDER], tiled=True)

    both = combine(at, legendre, got)
    pids = pair_of_slot.reshape(16, 8, 2, 2).transpose(0, 2, 1, 3).reshape(1, 512)
    place = jnp.where(pids % 2 == 0, pids, T_SIZE - pids) // 2
    t, tt, sign = slot_tables(place)
    spec, both, t, tt, sign = lax.optimization_barrier((spec, both, t, tt, sign))
    fold = jnp.asarray(fold_matrix(), BF)

    for step in range(STEPS):
        if step == 0:
            x = legendre_inverse(pair_of_slot, at, spec, both, variance, gauss_weight.reshape(1, 64))
        else:
            spec = lax.all_to_all(spec, "z", 0, 0, axis_index_groups=[ORDER], tiled=True)
            x = legendre_inverse(pair_of_slot, at, spec, both)
        x = lax.all_to_all(x, ("lat", "c"), 0, 0, tiled=True)
        if step == 0:
            y, var = grid_stage(x, fold, tt, t, sign, None)
        else:
            y = grid_stage(x, fold, tt, t, sign, var)
        y = lax.all_to_all(y, ("lat", "c"), 0, 0, tiled=True)
        parts = legendre_forward(pair_of_slot, at, y, both)
        parts = lax.all_to_all(parts, "z", 0, 0, axis_index_groups=[ORDER], tiled=True)
        if step + 1 < STEPS:
            spec = owner_step(parts, table)
    sh, gram = last_step(parts, table)
    grams = lax.all_to_all(gram.reshape(128, 1, 128), ("lat", "z"), 0, 0, tiled=True).reshape(128, 128)
    others = lax.ppermute(grams, "c", [(0, 1), (1, 0)])
    modes, lower = finish(sh, grams, others, table)
    return modes, lower[:, :K]


def solution(mesh):
    fine = Mesh(mesh.devices.reshape(16, 8, 2), ("lat", "z", "c"))
    placed = (
        P(("lat", "z", "c"), None, None, None),
        P("lat", ("z", "c"), None),
        P(("z", "c"), "lat"),
        P(("z", "c")),
        P(),
    )
    return jax.shard_map(
        body,
        mesh=fine,
        in_specs=placed,
        out_specs=(P(("lat", "z", "c"), None, None, None), P()),
        check_vma=False,
    )
```

```python
import functools
import math

import jax
import jax.numpy as jnp
import numpy as np
from jax import lax
from jax.experimental import pallas as pl
from jax.experimental.pallas import tpu as pltpu
from jax.sharding import Mesh
from jax.sharding import PartitionSpec as P

T_SIZE = 1023
NLON = 2048
K = 8
STEPS = 3
NPAIR = 512
R = 1025
RP = 1152
ORDER = [0, 1, 4, 5, 2, 3, 6, 7]
PLACE = [ORDER.index(i) for i in range(8)]
BF = jnp.bfloat16
F32 = jnp.float32
GSCALE = 1.0 / (2.0 * NPAIR * R)
SIGNS = np.array([[1, 1, 1, 1], [1, -1, 1, -1], [1, -1, -1, 1], [1, 1, -1, -1]], np.float32)


def natural_tables():
    q = np.arange(512)[:, None]
    i2 = 2 * np.arange(256)[None, :] + 1
    out = []
    for m in (2 * q, 1023 - 2 * q):
        angle = (m * i2 % 4096) * (2.0 * math.pi / 4096)
        out += [np.cos(angle), np.sin(angle)]
    return np.stack(out).astype(jnp.bfloat16)


def fold_matrix():
    f = np.zeros((4, 4, K, 4, 4, 4, K), np.float32)
    for jj in range(4):
        for g in range(4):
            for q in range(4):
                f[jj, g, :, g, q, jj, :] = SIGNS[g, q]
    return f.reshape(128, 512)


def lanes(shape):
    return lax.broadcasted_iota(jnp.int32, shape, len(shape) - 1)


def rows(shape):
    return lax.broadcasted_iota(jnp.int32, shape, len(shape) - 2)


def split_tile(g):
    hi = g.astype(BF).astype(F32)
    rest = g - hi
    mid = rest.astype(BF).astype(F32)
    low = (rest - mid).astype(BF).astype(F32)
    return hi + pltpu.roll(mid, 8, 1) + pltpu.roll(low, 16, 1)


def join_tile(t):
    g = t + pltpu.roll(t, 120, 1) + pltpu.roll(t, 112, 1)
    lane = lanes(t.shape)
    return jnp.where((lane >= 8) & (lane < 16) & (rows(t.shape) < 8), g, 0.0)


def splat_factor(gram):
    g = [[jnp.broadcast_to(gram[i : i + 1, j : j + 1] * GSCALE, (8, 128)) for j in range(i + 1)] for i in range(K)]
    low = [[None] * K for _ in range(K)]
    inv = [[None] * K for _ in range(K)]
    for j in range(K):
        d = g[j][j]
        for p in range(j):
            d = d - low[j][p] * low[j][p]
        r = lax.rsqrt(d)
        r = r * (1.5 - 0.5 * d * r * r)
        low[j][j] = d * r
        inv[j][j] = r
        for i in range(j + 1, K):
            v = g[i][j]
            for p in range(j):
                v = v - low[i][p] * low[j][p]
            low[i][j] = v * r
    for j in range(K):
        for i in range(j + 1, K):
            v = low[i][j] * inv[j][j]
            for p in range(j + 1, i):
                v = v + low[i][p] * inv[p][j]
            inv[i][j] = -(v * inv[i][i])
    return low, inv


def tile_of(entries, transposed, period):
    row, lane = rows((8, 128)), lanes((8, 128))
    if period:
        lane = lax.rem(lane, period)
    out = jnp.zeros((8, 128), F32)
    for i in range(K):
        for j in range(i + 1):
            r, l = (j, i) if transposed else (i, j)
            out = jnp.where((row == r) & (lane == l), entries[i][j], out)
    return out


def even_mask(shape, pid):
    first = (lanes(shape) < T_SIZE + 1 - pid).astype(jnp.int32)
    return first != lax.rem(pid, 2)


def load_block(ref, z, b):
    main = [ref[z, (b * 8 + l) * 16 : (b * 8 + l) * 16 + 16, :].astype(F32) for l in range(8)]
    extra = ref[z, 256:264, :].astype(F32)
    last = [pltpu.roll(extra, 128 - n, 1) if n else extra for n in (2 * b, 2 * b + 1)]
    last = jnp.concatenate(last, axis=0)
    return jnp.concatenate(main + [jnp.where(lanes((16, 128)) == 0, last, 0.0)], axis=1)


def pack(blocks, tile):
    lane = lanes((8, 128))
    pieces = [v[:, 128 * l : 128 * l + 128].astype(BF) for v in blocks for l in range(8)]
    for n in range(4):
        col = blocks[n // 2][8 * (n % 2) : 8 * (n % 2) + 8, 1024:RP]
        tile = jnp.where(lane == n, pltpu.roll(col, n, 1) if n else col, tile)
    return pieces + [tile.astype(BF)]


def put(out_ref, z, pieces):
    for n, v in enumerate(pieces):
        out_ref[z, 16 * n : 16 * n + v.shape[0], :] = v


def start_kernel(at_ref, start_ref, out_ref, table_ref):
    place, row = lanes((2, RP)), rows((2, RP))
    pid = jnp.where(row == 0, at_ref[2], at_ref[3])
    first = place < T_SIZE + 1 - pid
    degree = jnp.where(first, pid + place, place - 1)
    wave = jnp.where(first, pid, T_SIZE - pid)
    level = degree.astype(F32)
    scale = lax.rsqrt(1.0 + level * (level + 1.0) * (4.0 / (T_SIZE * T_SIZE)))
    scale = jnp.where(place < R, scale * (1.0 / NLON), 0.0)
    weight = jnp.where(wave == 0, 1.0, 2.0).astype(F32)
    phase = wave.astype(F32) * (2.0 * math.pi / (2 * NLON))
    cos, sin = jnp.cos(phase), jnp.sin(phase)
    table_ref[0:2, :] = scale
    table_ref[2:4, :] = weight
    table_ref[4:6, :] = cos
    table_ref[6:8, :] = sin
    lane = lanes((8, 128))
    blocks = []
    for b in range(2):
        half = []
        for c in range(2):
            col = jnp.broadcast_to(start_ref[b, :, c, 1024:R], (8, 128))
            half.append(jnp.concatenate([start_ref[b, :, c, 0:1024], jnp.where(lane == 0, col, 0.0)], axis=1))
        re, im = half
        cb, sb, wb = cos[b : b + 1], sin[b : b + 1], weight[b : b + 1]
        blocks.append(jnp.concatenate([wb * (re * cb + im * sb), wb * (re * sb - im * cb)], axis=0))
    pieces = pack(blocks, jnp.zeros((8, 128), F32))
    for z in range(out_ref.shape[0]):
        put(out_ref, z, pieces)


SMEM = pl.BlockSpec(memory_space=pltpu.SMEM)
VMEM = pl.BlockSpec(memory_space=pltpu.VMEM)
HBM = pl.BlockSpec(memory_space=pltpu.HBM)


def start_step(at, start):
    return pl.pallas_call(
        start_kernel,
        in_specs=[SMEM, VMEM],
        out_shape=(jax.ShapeDtypeStruct((8, 264, 128), BF), jax.ShapeDtypeStruct((8, RP), F32)),
        compiler_params=pltpu.CompilerParams(vmem_limit_bytes=12 << 20),
    )(at, start)


def table_kernel(place_ref, nat_ref, natt_ref, t_ref, tt_ref, sign_ref):
    hot = jnp.where(rows((512, 512)) == place_ref[...], 1.0, 0.0)
    hot_s = hot.T.astype(BF)
    hot = hot.astype(BF)
    for g in range(4):
        t_ref[512 * g : 512 * g + 512, :] = jnp.dot(hot_s, nat_ref[512 * g : 512 * g + 512, :], preferred_element_type=F32).astype(BF)
        tt_ref[:, 512 * g : 512 * g + 512] = jnp.dot(natt_ref[:, 512 * g : 512 * g + 512], hot, preferred_element_type=F32).astype(BF)
    turn = jnp.where(lax.rem(rows((512, 128)), 2) == 0, 1.0, -1.0).astype(BF)
    sign_ref[...] = jnp.dot(hot_s, turn, preferred_element_type=F32)


def slot_tables(place):
    nat = natural_tables()
    natt = np.ascontiguousarray(nat.transpose(2, 0, 1)).reshape(256, 2048)
    return pl.pallas_call(
        table_kernel,
        out_shape=(
            jax.ShapeDtypeStruct((2048, 256), BF),
            jax.ShapeDtypeStruct((256, 2048), BF),
            jax.ShapeDtypeStruct((512, 128), F32),
        ),
        compiler_params=pltpu.CompilerParams(vmem_limit_bytes=12 << 20),
    )(place, jnp.asarray(nat.reshape(2048, 256)), jnp.asarray(natt))


def slot_waves(spec_ref, z, b, pid, leg_ref, t):
    lane = lanes((32, 128))

    def own(pieces):
        return jnp.where(lane < 32, pieces[0], jnp.where(lane < 64, pieces[1], jnp.where(lane < 96, pieces[2], pieces[3])))

    main = [spec_ref[z, (b * 8 + l) * 16 : (b * 8 + l) * 16 + 16, :].astype(F32) for l in range(8)]
    sp = jnp.concatenate(main, axis=1)
    mask = even_mask((16, 1024), pid)
    even = jnp.where(mask, sp, 0.0).astype(BF)
    odd = jnp.where(mask, 0.0, sp).astype(BF)
    wide = jnp.concatenate([even, odd], axis=0)
    p = lax.dot_general(leg_ref[t, :, 0:1024], wide, (((1,), (1,)), ((), ())), preferred_element_type=F32)
    extra = spec_ref[z, 256:264, :].astype(F32)
    lane8, row8 = lanes((8, 128)), rows((8, 128))
    here = (lax.rem(lane8, 8) == row8) & (lax.rem(lane8 // 16, 2) == 1 - lax.rem(pid, 2))
    line = jnp.zeros((8, 128), F32)
    for c in range(2):
        col = jnp.broadcast_to(extra[:, 2 * b + c : 2 * b + c + 1], (8, 128))
        line = jnp.where(here & (lax.rem(lane8 // 8, 2) == c), col, line)
    line = jnp.sum(line, axis=0, keepdims=True)
    last = own([jnp.broadcast_to(leg_ref[t, 32 * jj : 32 * jj + 32, 1024:R].astype(F32), (32, 128)) for jj in range(4)])
    return jnp.concatenate([p[32 * jj : 32 * jj + 32] for jj in range(4)], axis=1) + last * line


def combine_kernel(at_ref, leg_ref, got_ref, both_ref, sems):
    core = at_ref[1]
    copies = []
    for z in range(8):
        for n, (ref, half) in enumerate(((leg_ref, core), (got_ref, 1 - core))):
            copy = pltpu.make_async_copy(
                ref.at[pl.ds(4 * z + 2 * core, 2)],
                both_ref.at[pl.ds(2 * z, 2), pl.ds(pl.multiple_of(half * 64, 64), 64)],
                sems.at[2 * z + n],
            )
            copy.start()
            copies.append(copy)
    for copy in copies:
        copy.wait()


def combine(at, leg, got):
    return pl.pallas_call(
        combine_kernel,
        in_specs=[SMEM, HBM, HBM],
        out_specs=HBM,
        out_shape=jax.ShapeDtypeStruct((16, 128, R), BF),
        scratch_shapes=[pltpu.SemaphoreType.DMA((16,))],
        compiler_params=pltpu.CompilerParams(vmem_limit_bytes=8 << 20),
    )(at, leg, got)


def whole(leg_ref, t):
    last = jnp.broadcast_to(leg_ref[t, :, 1024:R].astype(F32), (128, 128))
    last = jnp.where(lanes((128, 128)) == 0, last, 0.0).astype(BF)
    return jnp.concatenate([leg_ref[t, :, 0:1024], last], axis=1)


def inverse_kernel(first, pid_ref, at_ref, spec_ref, leg_ref, *refs):
    if first:
        var_ref, gauss_ref, out_ref, acc_ref = refs
        acc_ref[:, 16:24, :] = jnp.zeros((32, 8, 128), F32)
        gauss = jnp.broadcast_to(gauss_ref[...], (64, 64))
        gauss = jnp.sum(jnp.where(rows((64, 64)) == lanes((64, 64)), gauss, 0.0), axis=1, keepdims=True)
        rest = var_ref[...] * gauss
        for n in range(3):
            term = rest.astype(BF).astype(F32)
            rest = rest - term
            for jh in range(2):
                acc_ref[:, 16 + 2 * n + jh, :] = term[32 * jh : 32 * jh + 32, :]
    else:
        out_ref, acc_ref = refs
        tile = spec_ref[0, 256:264, :].astype(F32)
        for z in range(1, 8):
            tile = tile + spec_ref[z, 256:264, :].astype(F32)
        tile = split_tile(join_tile(tile)).astype(BF)
        out_ref[:, 16:24, :] = jnp.broadcast_to(tile[None], (32, 8, 128))
    for t in range(16):
        pid = pid_ref[at_ref[0] + 4 * (t // 2) + t % 2]
        acc_ref[:, t, :] = slot_waves(spec_ref, PLACE[t // 2], t % 2, pid, leg_ref, t)
    if first:
        out_ref[...] = acc_ref[...].astype(BF)
    else:
        out_ref[:, 0:16, :] = acc_ref[...].astype(BF)


def legendre_inverse(pids, at, spec, leg, *extra):
    first = len(extra) > 0
    return pl.pallas_call(
        functools.partial(inverse_kernel, first),
        in_specs=[SMEM, SMEM] + [VMEM] * (2 + len(extra)),
        out_shape=jax.ShapeDtypeStruct((32, 24, 128), BF),
        scratch_shapes=[pltpu.VMEM((32, 24 if first else 16, 128), F32)],
        compiler_params=pltpu.CompilerParams(vmem_limit_bytes=12 << 20),
    )(pids, at, spec, leg, *extra)


def arrange_variance(x_ref, b):
    row, lane = rows((128, 128)), lanes((128, 128))
    keep = jnp.where(row == lane, 1.0, 0.0).astype(BF)
    turn = jnp.where(row + lane == 127, 1.0, 0.0).astype(BF)
    er, el = rows((16, 128)), lanes((16, 128))
    used = (lax.rem(er, 8) < 6) & (lax.rem(el, 32) // 8 == 2 * (er // 8) + lax.rem(er, 2))
    halves = []
    for places in (
        ((b, keep), (7 - b, turn), (8 + b, keep), (15 - b, turn)),
        ((3 - b, turn), (4 + b, keep), (11 - b, turn), (12 + b, keep)),
    ):
        total = None
        for q, (a, order) in enumerate(places):
            terms = jnp.concatenate([x_ref[2 * a, 16:24, :], x_ref[2 * a + 1, 16:24, :]], axis=0)
            down = lax.dot_general(order, terms, (((1,), (1,)), ((), ())), preferred_element_type=F32).astype(BF)
            spread = jnp.where(used & (el // 32 == q), 1.0, 0.0).astype(BF)
            part = jnp.dot(down, spread, preferred_element_type=F32)
            total = part if total is None else total + part
        halves.append(total)
    return jnp.concatenate(halves, axis=1)


def grid_kernel(first, x_ref, fold_ref, tt_ref, t_ref, sign_ref, *refs):
    x = x_ref[:, 0:16, :].reshape(512, 128)
    if first:
        y_ref, var_ref, hat_ref = refs
        for b in range(2):
            var_ref[128 * b : 128 * b + 128, :] = arrange_variance(x_ref, b)
    else:
        var_ref, y_ref, hat_ref = refs
        tile = jnp.sum(x_ref[:, 16:24, :].astype(F32), axis=0)
        gram = pltpu.roll(join_tile(tile), 120, 1)
        mix = tile_of(splat_factor(gram)[1], True, K)
        mix = jnp.concatenate([mix] * 16, axis=0)
    sign = sign_ref[...]
    for g in range(4):
        f = fold_ref[:, 128 * g : 128 * g + 128].astype(F32)
        if first:
            f = jnp.where(lax.rem(rows((128, 128)), 8) == lax.rem(lanes((128, 128)), 8), f, 0.0)
            hat = jnp.dot(x, f.astype(BF), preferred_element_type=F32)
        else:
            f = f * mix
            hi = f.astype(BF)
            low = (f - hi.astype(F32)).astype(BF)
            hat = jnp.dot(x, hi, preferred_element_type=F32) + jnp.dot(x, low, preferred_element_type=F32)
        turned = hat * sign if g == 0 else hat * -sign
        to = (0, 1, 3, 2)[g]
        hat_ref[512 * g : 512 * g + 512, 0:128] = hat.astype(BF)
        hat_ref[512 * to : 512 * to + 512, 128:256] = turned.astype(BF)
    grid = jnp.dot(tt_ref[...], hat_ref[...], preferred_element_type=F32)
    scaled = (grid * var_ref[...]).astype(BF)
    lane = lanes((1, 128))
    parts = [jnp.dot(t_ref[512 * g : 512 * g + 512, :], scaled, preferred_element_type=F32) for g in range(4)]
    out = None
    for g in range(4):
        turned = parts[(0, 1, 3, 2)[g]][:, 128:256]
        part = parts[g][:, 0:128] + (turned * sign if g == 0 else turned * -sign)
        flip = jnp.ones((1, 128), F32)
        for q in range(4):
            if SIGNS[g, q] < 0:
                flip = jnp.where((lane >= 32 * q) & (lane < 32 * q + 32), -1.0, flip)
        part = part * flip
        part = part + pltpu.roll(part, 64, 1)
        part = part + pltpu.roll(part, 32, 1)
        out = part if out is None else jnp.where(lane >= 32 * g, part, out)
    y_ref[...] = out.astype(BF).reshape(32, 16, 128)


def grid_stage(x, fold, tt, t, sign, var):
    first = var is None
    y = jax.ShapeDtypeStruct((32, 16, 128), BF)
    return pl.pallas_call(
        functools.partial(grid_kernel, first),
        out_shape=(y, jax.ShapeDtypeStruct((256, 256), F32)) if first else y,
        scratch_shapes=[pltpu.VMEM((2048, 256), BF)],
        compiler_params=pltpu.CompilerParams(vmem_limit_bytes=12 << 20),
    )(*((x, fold, tt, t, sign) if first else (x, fold, tt, t, sign, var)))


def forward_kernel(pid_ref, at_ref, y_ref, leg_ref, out_ref, wide_ref):
    wide_ref[...] = y_ref[...].astype(F32)
    lane = lanes((32, 128))
    for b in range(4):
        zt = jnp.concatenate([wide_ref[:, 4 * b + s, :] for s in range(4)], axis=0).T
        blocks = [
            jnp.concatenate([zt[32 * g + 8 * jj : 32 * g + 8 * jj + 8, :] for g in range(4)], axis=0)
            for jj in range(4)
        ]
        done = []
        for s in range(4):
            t = 4 * b + s
            lhs = None
            for jj in range(4):
                shift = (32 * (jj - s)) % 128
                v = pltpu.roll(blocks[jj], shift, 1) if shift else blocks[jj]
                lhs = v if lhs is None else jnp.where(lane >= 32 * jj, v, lhs)
            p = jnp.dot(lhs.astype(BF), whole(leg_ref, t), preferred_element_type=F32)
            mask = even_mask((16, RP), pid_ref[at_ref[0] + 4 * (t // 2) + t % 2])
            done.append(jnp.where(mask, p[0:16], p[16:32]))
        for u in range(2):
            put(out_ref, PLACE[2 * b + u], pack(done[2 * u : 2 * u + 2], jnp.zeros((8, 128), F32)))


def legendre_forward(pids, at, y, leg):
    return pl.pallas_call(
        forward_kernel,
        in_specs=[SMEM, SMEM, VMEM, VMEM],
        out_shape=jax.ShapeDtypeStruct((8, 264, 128), BF),
        scratch_shapes=[pltpu.VMEM((32, 16, 128), F32)],
        compiler_params=pltpu.CompilerParams(vmem_limit_bytes=12 << 20),
    )(pids, at, y, leg)


def gram_tile(blocks):
    sh = jnp.concatenate(blocks, axis=0)
    hi = sh.astype(BF)
    low = (sh - hi.astype(F32)).astype(BF)
    both = jnp.concatenate([hi, low, jnp.zeros((64, RP), BF)], axis=0)
    full = lax.dot_general(both[0:64], both, (((1,), (1,)), ((), ())), preferred_element_type=F32)
    total = None
    for a in range(2):
        for b in range(2):
            for i in range(4):
                v = full[32 * a + 8 * i : 32 * a + 8 * i + 8, :]
                shift = (128 - (32 * b + 8 * i)) % 128
                v = pltpu.roll(v, shift, 1) if shift else v
                total = v if total is None else total + v
    return jnp.where(lanes((8, 128)) < 8, total, 0.0)


def summed_blocks(parts_ref, table_ref):
    out = []
    for b in range(2):
        total = load_block(parts_ref, 0, b)
        for z in range(1, parts_ref.shape[0]):
            total = total + load_block(parts_ref, z, b)
        out.append(total * table_ref[b : b + 1, :])
    return out


def owner_kernel(parts_ref, table_ref, out_ref):
    sh = summed_blocks(parts_ref, table_ref)
    tile = split_tile(pltpu.roll(gram_tile(sh), 8, 1))
    pieces = pack([sh[b] * table_ref[2 + b : 3 + b, :] for b in range(2)], tile)
    for z in range(out_ref.shape[0]):
        put(out_ref, z, pieces)


def owner_step(parts, table):
    return pl.pallas_call(
        owner_kernel,
        out_shape=jax.ShapeDtypeStruct((8, 264, 128), BF),
        compiler_params=pltpu.CompilerParams(vmem_limit_bytes=12 << 20),
    )(parts, table)


def last_kernel(parts_ref, table_ref, sh_ref, gram_ref):
    sh = summed_blocks(parts_ref, table_ref)
    for b in range(2):
        sh_ref[16 * b : 16 * b + 16, :] = sh[b]
    tile = gram_tile(sh)
    line = tile[0:1, :]
    for i in range(1, K):
        line = line + pltpu.roll(tile[i : i + 1, :], 8 * i, 1)
    gram_ref[...] = jnp.broadcast_to(line, gram_ref.shape)


def last_step(parts, table):
    return pl.pallas_call(
        last_kernel,
        out_shape=(jax.ShapeDtypeStruct((32, RP), F32), jax.ShapeDtypeStruct((128, 128), F32)),
        compiler_params=pltpu.CompilerParams(vmem_limit_bytes=12 << 20),
    )(parts, table)


def finish_kernel(sh_ref, gram_ref, other_ref, table_ref, modes_ref, lower_ref):
    line = jnp.sum(gram_ref[...] + other_ref[...], axis=0, keepdims=True)
    row = rows((8, 128))
    gram = jnp.broadcast_to(line, (8, 128))
    for i in range(1, K):
        gram = jnp.where(row == i, jnp.broadcast_to(pltpu.roll(line, 128 - 8 * i, 1), (8, 128)), gram)
    low, inv = splat_factor(gram)
    lower_ref[...] = tile_of(low, False, 0)
    coefs = []
    for q in range(K):
        coef = jnp.zeros((8, 128), F32)
        for i in range(q, K):
            coef = jnp.where(row == i, inv[i][q], coef)
        coefs.append(jnp.concatenate([coef] * (RP // 128), axis=1))
    for b in range(2):
        cos, sin = table_ref[4 + b : 5 + b, :], table_ref[6 + b : 7 + b, :]
        parts = []
        for c in range(2):
            block = sh_ref[16 * b + 8 * c : 16 * b + 8 * c + 8, :]
            out = coefs[0] * block[0:1, :]
            for q in range(1, K):
                out = out + coefs[q] * block[q : q + 1, :]
            parts.append(out)
        for c, v in enumerate((cos * parts[0] + sin * parts[1], sin * parts[0] - cos * parts[1])):
            modes_ref[b, :, c, 0:1024] = v[:, 0:1024]
            modes_ref[b, :, c, 1024:R] = v[:, 1024:R]


def finish(sh, grams, others, table):
    return pl.pallas_call(
        finish_kernel,
        out_shape=(jax.ShapeDtypeStruct((2, K, 2, R), F32), jax.ShapeDtypeStruct((8, 128), F32)),
        compiler_params=pltpu.CompilerParams(vmem_limit_bytes=12 << 20),
    )(sh, grams, others, table)


def body(start_block, legendre, variance, gauss_weight, pair_of_slot):
    lat, zpos, core = lax.axis_index("lat"), lax.axis_index("z"), lax.axis_index("c")
    base = lat * 32 + core * 2
    own = lax.dynamic_slice(pair_of_slot, (base + zpos * 4,), (2,))
    at = jnp.concatenate([jnp.stack([base, core]).astype(jnp.int32), own])
    got = lax.ppermute(legendre, "c", [(0, 1), (1, 0)])
    spec, table = start_step(at, start_block)
    spec = lax.all_to_all(spec, "z", 0, 0, axis_index_groups=[ORDER], tiled=True)

    both = combine(at, legendre, got)
    pids = pair_of_slot.reshape(16, 8, 2, 2).transpose(0, 2, 1, 3).reshape(1, 512)
    place = jnp.where(pids % 2 == 0, pids, T_SIZE - pids) // 2
    t, tt, sign = slot_tables(place)
    spec, both, t, tt, sign = lax.optimization_barrier((spec, both, t, tt, sign))
    fold = jnp.asarray(fold_matrix(), BF)

    for step in range(STEPS):
        if step == 0:
            x = legendre_inverse(pair_of_slot, at, spec, both, variance, gauss_weight.reshape(1, 64))
        else:
            spec = lax.all_to_all(spec, "z", 0, 0, axis_index_groups=[ORDER], tiled=True)
            x = legendre_inverse(pair_of_slot, at, spec, both)
        x = lax.all_to_all(x, ("lat", "c"), 0, 0, tiled=True)
        if step == 0:
            y, var = grid_stage(x, fold, tt, t, sign, None)
        else:
            y = grid_stage(x, fold, tt, t, sign, var)
        y = lax.all_to_all(y, ("lat", "c"), 0, 0, tiled=True)
        parts = legendre_forward(pair_of_slot, at, y, both)
        parts = lax.all_to_all(parts, "z", 0, 0, axis_index_groups=[ORDER], tiled=True)
        if step + 1 < STEPS:
            spec = owner_step(parts, table)
    sh, gram = last_step(parts, table)
    grams = lax.all_to_all(gram.reshape(128, 1, 128), ("lat", "z"), 0, 0, tiled=True).reshape(128, 128)
    others = lax.ppermute(grams, "c", [(0, 1), (1, 0)])
    modes, lower = finish(sh, grams, others, table)
    return modes, lower[:, :K]


def solution(mesh):
    fine = Mesh(mesh.devices.reshape(16, 8, 2), ("lat", "z", "c"))
    placed = (
        P(("lat", "z", "c"), None, None, None),
        P("lat", ("z", "c"), None),
        P(("z", "c"), "lat"),
        P(("z", "c")),
        P(),
    )
    return jax.shard_map(
        body,
        mesh=fine,
        in_specs=placed,
        out_specs=(P(("lat", "z", "c"), None, None, None), P()),
        check_vma=False,
    )
```
